256 devices in a mesh: blk: 16 (over y_lo, z), tp: 4 (over y_hi, core), dp: 4 (over x).
Axes of the slice: x: 4, y: 4 (y_hi: 2, y_lo: 2; y = y_hi * 2 + y_lo), z: 8, core: 2. Of those that a mesh axis runs over, the one named last changes fastest.
Arguments:
- layer_input: bfloat16 [24576, 8192], P(('blk', 'dp')), may hold values from -16 to 16
- queries: bfloat16 [24576, 4096], P(('blk', 'dp'), 'tp'), may hold values from -160 to 160
- keys: bfloat16 [24576, 512], P(('blk', 'dp'), 'tp'), may hold values from -7 to 7
- values: bfloat16 [24576, 512], P(('blk', 'dp'), 'tp'), may hold values from -6 to 6
- kv_weight: bfloat16 [8192, 1024], P('blk', 'tp'), may hold values from -0.0625 to 0.0625
- out_grad: bfloat16 [24576, 4096], P(('blk', 'dp'), 'tp'), may hold values from -6 to 6
- doc_lengths: int32 [64, 4], P(('blk', 'dp')), may hold values from 1 to 192, 384 in all within a row
Outputs:
- input_grad: bfloat16 [24576, 8192], P(('blk', 'dp'), 'tp')
- query_grad: bfloat16 [24576, 4096], P(('blk', 'dp'), 'tp')
- weight_grad: float32 [8192, 1024], P('blk', 'tp')
The draws below stay inside these ranges and needn't reach their ends.
All inputs are finite; a program needn't handle non-finite values.
Results may differ from the reference program's by a relative error of at most 0.015.
Values may be sent and summed in bfloat16 or wider, within the bound.
A program may use at most 128 MiB of HBM per device.

```python
import math
import jax
import jax.numpy as jnp
import numpy as np
from jax import lax

D = 8192
HD = 128
QH = 32
KVH = 4
GROUP = 8
TOK_DEV = 384
DOCS = 4
WORKERS = 64
TOKENS = 24576


def shared_keys(key):
    return jnp.clip(jax.random.normal(key, (TOKENS, KVH * HD), jnp.float32), -6.5, 6.5)


def draw_keys(key, part):
    base = shared_keys(key)
    return base.astype(jnp.bfloat16)


def draw_queries(key, part):
    key = jax.random.fold_in(key, 11)
    first_key = jax.random.fold_in(key, 0)
    drawn = jnp.clip(jax.random.normal(first_key, (TOKENS, QH * HD), jnp.float32), -6.0, 6.0)
    return drawn.astype(jnp.bfloat16)


def spiked(entries, key, source, target, blocks, factor):
    def block_of(dim):
        return (jnp.arange(entries.shape[dim]) // (entries.shape[dim] // blocks)).reshape((-1,) + (1,) * (entries.ndim - 1 - dim))

    first = jax.random.permutation(key, blocks)[block_of(target)]
    other_side = (block_of(target) + blocks // 2) % blocks
    return jnp.where((block_of(source) == first) | (block_of(source) == other_side), factor * entries, entries)


def block_levels(rng, shape, pieces, least, top_value):
    def one(dim, shards_of):
        heights = jax.random.uniform(jax.random.fold_in(jax.random.fold_in(rng, 6), dim), (shards_of,), jnp.float32, least / len(pieces), top_value / len(pieces))
        return jnp.repeat(jnp.exp(heights), shape[dim] // shards_of).reshape((-1,) + (1,) * (len(shape) - dim - 1))

    loudness = one(*pieces[0])
    for cut in pieces[1:]:
        loudness = loudness * one(*cut)
    return loudness


def profile(count, total, most, skew):
    loads = [(1 << 20) // math.isqrt(standing ** skew) + 1 for standing in range(2, count + 1)]
    surplus, holding = total - most - (count - 1), [1] * (count - 1)
    while surplus > 0:
        movable = [i for i in range(count - 1) if holding[i] < most]
        whole, left = sum([loads[i] for i in movable]), surplus
        for i in movable:
            addition = min(most - holding[i], max(1, left * loads[i] // whole), surplus)
            holding[i] = holding[i] + addition
            surplus = surplus - addition
    return np.array([most] + holding)


def uneven(rng, number_of, total, most, lean):
    if number_of == 2:
        one = jax.random.randint(rng, (), max(1, total - most), min(most, total - 1) + 1)
        return jnp.stack([one, total - one])
    tallies = jnp.asarray(profile(number_of, total, most, lean), jnp.int32)
    pairs = (number_of - 1) // 2
    donor, taker = tallies[1:1 + 2 * pairs:2], tallies[2:2 + 2 * pairs:2]
    slack = jnp.minimum(donor - 1, most - taker)
    moved = jax.random.randint(jax.random.fold_in(rng, 1), (pairs,), 0, 1 << 20) % (slack + 1)
    tallies = tallies.at[1:1 + 2 * pairs:2].set(donor - moved).at[2:2 + 2 * pairs:2].set(taker + moved)
    return tallies[jax.random.permutation(jax.random.fold_in(rng, 2), number_of)]


def normal_values(stream_key, dims, width, reach, pieces=(), kind=jnp.bfloat16):
    result = width * jax.random.normal(stream_key, dims, jnp.float32)
    if pieces:
        result = result * block_levels(stream_key, dims, pieces, -0.22, 0.18)
    return jnp.clip(result, -reach, reach).astype(kind)


def noise_with(stream_key, extent, scale, limit, cuts, heavy, held_as=jnp.bfloat16):
    array = scale * jax.random.normal(stream_key, extent, jnp.float32)
    if cuts:
        array = array * block_levels(stream_key, extent, cuts, -0.22, 0.18)
    return jnp.clip(spiked(array, jax.random.fold_in(stream_key, 3), *heavy), -limit, limit).astype(held_as)


def setup_inputs(seed: int = 0) -> dict:
    streams_of = jax.random.split(jax.random.key(seed), 8)
    layer_input = noise_with(streams_of[0], (TOKENS, D), 1.0, 16.0, ((0, 64),), (0, 1, 64, 4.0))
    queries = draw_queries(jax.random.fold_in(streams_of[7], 71), 0)
    keys = draw_keys(jax.random.fold_in(streams_of[7], 71), 0)
    values = normal_values(streams_of[3], (TOKENS, KVH * HD), 1.0, 6.0, ((0, 64), (1, 4)))
    kv_weight = normal_values(streams_of[4], (D, KVH * 2 * HD), D ** -0.5, 0.0625, ((0, 16), (1, 4)))
    out_grad = normal_values(streams_of[5], (TOKENS, QH * HD), 1.0, 6.0, ((0, 64), (1, 4)))
    doc_lengths = jax.vmap(lambda own: uneven(own, DOCS, TOK_DEV, TOK_DEV // 2, 2))(jax.random.split(streams_of[6], WORKERS)).reshape((WORKERS, DOCS)).astype(jnp.int32)
    return dict(layer_input=layer_input, queries=queries, keys=keys, values=values, kv_weight=kv_weight, out_grad=out_grad, doc_lengths=doc_lengths)


def attend_back(query_rows, key_rows, value_rows, grad_rows, lengths):
    query_heads = query_rows.astype(jnp.float32).reshape(TOK_DEV, KVH, GROUP, HD)
    key_heads = key_rows.astype(jnp.float32).reshape(TOK_DEV, KVH, HD)
    value_heads = value_rows.astype(jnp.float32).reshape(TOK_DEV, KVH, HD)
    grad_heads = grad_rows.astype(jnp.float32).reshape(TOK_DEV, KVH, GROUP, HD)
    positions = jnp.arange(TOK_DEV, dtype=jnp.int32)
    doc_ends = jnp.cumsum(lengths)
    documents = jnp.sum((positions[:, None] >= doc_ends[None, :]).astype(jnp.int32), axis=1)
    allowed = (documents[:, None] == documents[None, :]) & (positions[None, :] <= positions[:, None])
    score_scale = 1.0 / (HD ** 0.5)
    scores = jnp.einsum("ikgd,jkd->kgij", query_heads, key_heads) * score_scale
    scores = jnp.where(allowed[None, None], scores, -1e30)
    peaks = jnp.max(scores, axis=-1, keepdims=True)
    powers = jnp.exp(scores - peaks)
    soft_probs = powers / jnp.sum(powers, axis=-1, keepdims=True)
    probs_low = soft_probs.astype(jnp.bfloat16)
    prob_grad = jnp.einsum("ikgd,jkd->kgij", grad_heads, value_heads)
    inner = jnp.sum(soft_probs * prob_grad, axis=-1, keepdims=True)
    score_grad = (soft_probs * (prob_grad - inner) * score_scale).astype(jnp.bfloat16).astype(jnp.float32)
    query_grad = jnp.einsum("kgij,jkd->ikgd", score_grad, key_heads).astype(jnp.bfloat16)
    key_grad = jnp.einsum("kgij,ikgd->jkd", score_grad, query_heads)
    value_grad = jnp.einsum("kgij,ikgd->jkd", probs_low.astype(jnp.float32), grad_heads)
    kv_grad = jnp.stack([key_grad, value_grad], axis=2).astype(jnp.bfloat16).reshape(TOK_DEV, KVH * 2 * HD)
    return query_grad.reshape(TOK_DEV, QH * HD), kv_grad


def reference(layer_input, queries, keys, values, kv_weight, out_grad, doc_lengths):
    inputs_w = layer_input.reshape(WORKERS, TOK_DEV, D)
    queries_w = queries.reshape(WORKERS, TOK_DEV, QH * HD)
    keys_w = keys.reshape(WORKERS, TOK_DEV, KVH * HD)
    values_w = values.reshape(WORKERS, TOK_DEV, KVH * HD)
    grads_w = out_grad.reshape(WORKERS, TOK_DEV, QH * HD)

    def one_worker(total, items):
        rows_in, rows_q, rows_k, rows_v, rows_g, lengths = items
        query_grad, kv_grad = attend_back(rows_q, rows_k, rows_v, rows_g, lengths)
        input_grad = lax.dot_general(kv_grad, kv_weight, (((1,), (1,)), ((), ())),
                                     preferred_element_type=jnp.float32).astype(jnp.bfloat16)
        term = lax.dot_general(rows_in, kv_grad, (((0,), (0,)), ((), ())),
                               preferred_element_type=jnp.float32)
        return total + term, (input_grad, query_grad)

    start_total = jnp.zeros((D, KVH * 2 * HD), jnp.float32)
    weight_grad, outputs = lax.scan(one_worker, start_total,
                                    (inputs_w, queries_w, keys_w, values_w, grads_w, doc_lengths))
    input_grad = outputs[0].reshape(TOKENS, D)
    query_grad = outputs[1].reshape(TOKENS, QH * HD)
    return input_grad, query_grad, weight_grad
```

```python
import functools

import jax
import jax.numpy as jnp
from jax import lax
from jax.experimental import pallas as pl
from jax.experimental.pallas import tpu as pltpu
from jax.sharding import PartitionSpec as P

HD = 128
MESH = pl.DeviceIdType.MESH
F32 = jnp.float32
BF16 = jnp.bfloat16


def device(x, y, z, c):
    return {"blk": (y % 2) * 8 + z, "tp": (y // 2) * 2 + c, "dp": x}


def dot(a, b, dims):
    return lax.dot_general(a, b, (dims, ((), ())), preferred_element_type=F32)


def kernel(
    li, q, k, v, w, do, dl,
    ig, qg, wg,
    xb, wz, wfull, kv_all, kv_oth, kvt, sbuf, rbuf, facc, xs, xr, fin, wgt, bias, kacc, vacc,
    xo_sem, xs_s, xs_r, xsib_s, xsib_r,
    w0_s, w0_r, wz_s, wz_r, wx_s, wx_r, wsib_s, wsib_r, wloc,
    k1_s, k1_r, k2_s, k2_r, ks_s, ks_r,
    rs_s, rs_r, xr_s, xr_r, fin_s, fin_r,
):
    blk, tp, x = lax.axis_index("blk"), lax.axis_index("tp"), lax.axis_index("dp")
    yl, z, yh, c = blk // 8, blk % 8, tp // 2, tp % 2
    y = yh * 2 + yl
    p = x % 2

    def remote(src, dst, ssem, rsem, dev):
        return pltpu.make_async_remote_copy(
            src_ref=src, dst_ref=dst, send_sem=ssem, recv_sem=rsem,
            device_id=dev, device_id_type=MESH,
        )

    def at(dx=0, dy=0, dz=0, core=None):
        return device((x + dx) % 4, (y + dy) % 4, (z + dz) % 8, c if core is None else core)

    sibling = at(core=1 - c)

    partners = [at(dz=1), at(dz=7), sibling, at(dy=1), at(dy=2), at(dy=3), at(dx=2)]
    for dx in (1, 3):
        for core in (0, 1):
            partners.append(at(dx=dx, core=core))
    for dx in (1, 2, 3):
        for dy in (1, 3):
            partners.append(at(dx=dx, dy=dy))
    barrier = pltpu.get_barrier_semaphore()
    for d in partners:
        pl.semaphore_signal(barrier, inc=1, device_id=d, device_id_type=MESH)

    def x_own(zp):
        cols = pl.ds(pl.multiple_of(((1 - yl) * 8 + zp) * 512 + yh * 256, 256), 256)
        return pltpu.make_async_copy(li.at[:, cols], xb.at[zp, pl.ds(0, 384)], xo_sem.at[zp])

    for zp in range(8):
        x_own(zp).start()

    pl.semaphore_wait(barrier, len(partners))

    rows_p = pl.ds(pl.multiple_of(p * 256, 256), 256)

    def w0_remote(i):
        return remote(
            w.at[rows_p], wz.at[z, yh], w0_s.at[i], w0_r.at[yh],
            device(x, 2 * yl + i, z, c),
        )

    def w0_local(i):
        return pltpu.make_async_copy(w.at[rows_p], wz.at[z, yh], w0_r.at[yh])

    for i in range(2):
        @pl.when(2 * yl + i != y)
        def _():
            w0_remote(i).start()

        @pl.when(2 * yl + i == y)
        def _():
            w0_local(i).start()

    def x_send(side, j):
        ydst = (y + 1) % 4 if side == 0 else (y + 3) % 4
        zp = 4 * c + j
        cols = pl.ds(pl.multiple_of((yl * 8 + zp) * 512 + (ydst // 2) * 256, 256), 256)
        return remote(
            li.at[pl.ds(192 * side, 192), cols],
            xb.at[zp, pl.ds(384 + 192 * side, 192)],
            xs_s.at[side, j], xs_r.at[side, j], device(x, ydst, z, c),
        )

    for j in range(4):
        for side in range(2):
            x_send(side, j).start()

    def x_relay():
        mine = pl.ds(4 * c, 4)
        return remote(
            xb.at[mine, pl.ds(384, 384)], xb.at[mine, pl.ds(384, 384)],
            xsib_s, xsib_r, sibling,
        )

    def spread_x(zp, side):
        j, cz = zp % 4, zp // 4
        return remote(
            wz.at[zp, side], wfull.at[j, c, side, rows_p],
            wx_s.at[zp, side], wx_r.at[j, c, side],
            at(dx=1 if side == 0 else 3, core=cz),
        )

    def spread_sibling(zp):
        j = zp % 4
        return remote(
            wz.at[zp], wfull.at[j, c, :, rows_p], wsib_s.at[zp], wsib_r.at[j], sibling
        )

    def spread_local(zp):
        j = zp % 4
        return pltpu.make_async_copy(wz.at[zp], wfull.at[j, c, :, rows_p], wloc.at[j])

    def spread(zp):
        for side in range(2):
            spread_x(zp, side).start()

        @pl.when(zp // 4 == c)
        def _():
            spread_local(zp).start()

        @pl.when(zp // 4 != c)
        def _():
            spread_sibling(zp).start()

    def wz_copy(direction, s):
        zp = (z - s + 8) % 8 if direction == 0 else (z + s) % 8
        ref = wz.at[zp, direction] if s == 3 else wz.at[zp]
        return remote(
            ref, ref, wz_s.at[direction, s], wz_r.at[direction, s],
            at(dz=1 if direction == 0 else 7),
        )

    def wz_wait(direction, s):
        zp = (z - s + 7) % 8 if direction == 0 else (z + s + 1) % 8
        ref = wz.at[zp, direction] if s == 3 else wz.at[zp]
        remote(ref, ref, wz_s.at[direction, s], wz_r.at[direction, s], sibling).wait_recv()
        return zp

    def w_begin():
        for h in range(2):
            remote(w.at[rows_p], wz.at[z, h], w0_s.at[h], w0_r.at[h], sibling).wait_recv()
        for direction in range(2):
            wz_copy(direction, 0).start()
        spread(z)

    def w_step(s):
        arrived = [wz_wait(direction, s) for direction in range(2)]
        if s < 3:
            for direction in range(2):
                wz_copy(direction, s + 1).start()
            for zp in arrived:
                spread(zp)
        else:
            spread(arrived[0])

    lens = [dl[0, i] for i in range(3)]
    ends = [lens[0], lens[0] + lens[1], lens[0] + lens[1] + lens[2]]

    def documents(shape, dim):
        pos = lax.broadcasted_iota(jnp.int32, shape, dim)
        return pos, sum((pos >= e).astype(jnp.int32) for e in ends)

    kpos, kdoc = documents((384, 1), 0)
    qpos, qdoc = documents((1, 384), 1)
    bias[...] = jnp.where((kdoc == qdoc) & (kpos <= qpos), 0.0, -1e30).astype(F32)
    kacc[...] = jnp.zeros_like(kacc)
    vacc[...] = jnp.zeros_like(vacc)
    scale = 1.0 / HD**0.5

    def head(h, carry):
        lanes = pl.ds(pl.multiple_of(h * HD, HD), HD)
        for b in range(3):
            n = 128 * (b + 1)
            rows = pl.ds(128 * b, 128)
            qb, gb = q[rows, lanes], do[rows, lanes]
            s = dot(k[:n], qb, ((1,), (1,))) + bias[:n, 128 * b:n]
            e = jnp.exp((s - jnp.max(s, axis=0, keepdims=True)) * scale)
            probs = e * (1.0 / jnp.sum(e, axis=0, keepdims=True))
            pg = dot(v[:n], gb, ((1,), (1,)))
            inner = jnp.sum(probs * pg, axis=0, keepdims=True)
            ds = (probs * (pg - inner) * scale).astype(BF16)
            qg[rows, lanes] = dot(ds, k[:n], ((0,), (0,))).astype(BF16)
            kacc[:n] += dot(ds, qb, ((1,), (0,)))
            vacc[:n] += dot(probs.astype(BF16), gb, ((1,), (0,)))
        return carry

    lax.fori_loop(0, 2, head, 0)
    w_begin()
    lax.fori_loop(2, 8, head, 0)

    kv_all[c, yh, :, :HD] = kacc[...].astype(BF16)
    kv_all[c, yh, :, HD:] = vacc[...].astype(BF16)

    def kv1(side):
        return remote(
            kv_all.at[c, yh], kv_oth.at[yh], k1_s.at[side], k1_r.at[yh],
            at(dy=1 if side == 0 else 3),
        )

    for side in range(2):
        kv1(side).start()

    def kv_sibling(i):
        ref = kv_all.at[c, yh] if i == 0 else kv_all.at[c, 1 - yh]
        return remote(ref, ref, ks_s.at[i], ks_r.at[i], sibling)

    kv_sibling(0).start()

    def kv2(side):
        hsrc = ((y + 3) % 4) // 2 if side == 0 else ((y + 1) % 4) // 2
        rows = pl.ds(192 * side, 192)
        return remote(
            kv_oth.at[hsrc, rows], kv_all.at[c, hsrc, rows], k2_s.at[side], k2_r.at[side],
            at(dy=1 if side == 0 else 3),
        )

    def transpose_kv(h):
        kvt[h, :, :384] = kv_all[c, h].astype(F32).T.astype(BF16)
        kvt[h, :, 384:] = kv_oth[h].astype(F32).T.astype(BF16)

    def partial(h, zp, rows=slice(None)):
        return dot(kvt[h, rows, :], xb[zp], ((1,), (0,)))

    def rs_copy(f, direction, s):
        half = pl.ds(0, 128) if s == 0 else pl.ds(0, 256)
        return remote(
            sbuf.at[f, direction, s, half], rbuf.at[f, direction, s, half],
            rs_s.at[f, direction, s], rs_r.at[f, direction, s],
            at(dz=1 if direction == 0 else 7),
        )

    def rs_step(f, s):
        h = yh if f == 0 else 1 - yh
        terms = []
        for direction in range(2):
            zd = (z + 4 - s) % 8 if direction == 0 else (z + 4 + s) % 8
            if s == 0:
                terms.append(partial(h, zd, slice(128 * direction, 128 * direction + 128)))
            else:
                terms.append(partial(h, zd))
        for direction in range(2):
            if s == 0:
                sbuf[f, direction, 0, :128] = terms[direction].astype(BF16)
            else:
                rs_copy(f, direction, s - 1).wait_recv()
                if s == 1:
                    mine = slice(128 * direction, 128 * direction + 128)
                    rest = slice(128 - 128 * direction, 256 - 128 * direction)
                    sbuf[f, direction, 1, rest] = terms[direction][rest].astype(BF16)
                    sbuf[f, direction, 1, mine] = (
                        terms[direction][mine] + rbuf[f, direction, 0, :128].astype(F32)
                    ).astype(BF16)
                else:
                    sbuf[f, direction, s] = (
                        terms[direction] + rbuf[f, direction, s - 1].astype(F32)
                    ).astype(BF16)
            rs_copy(f, direction, s).start()

    def x_copy(f, i):
        quarter = pl.ds(pl.multiple_of(((x + i) % 4) * 64, 64), 64)
        return remote(
            xs.at[f, quarter], xr.at[f, i - 1], xr_s.at[f, i - 1], xr_r.at[f, i - 1], at(dx=i)
        )

    def rs_last(f):
        h = yh if f == 0 else 1 - yh
        total = partial(h, z)
        for direction in range(2):
            rs_copy(f, direction, 3).wait_recv()
            total = total + rbuf[f, direction, 3].astype(F32)
        facc[f] = total
        xs[f] = total.astype(BF16)
        for i in (2, 1, 3):
            x_copy(f, i).start()

    def fin_copy(f, i):
        h = yh if f == 0 else 1 - yh
        cols = pl.ds(pl.multiple_of(x * 64, 64), 64)
        return remote(
            fin.at[f], wgt.at[yh, cols], fin_s.at[f, i], fin_r.at[yh, x],
            device((x + i) % 4, 2 * h + 1 - yl, z, c),
        )

    def x_last(f):
        total = facc[f, pl.ds(pl.multiple_of(x * 64, 64), 64)]
        for i in range(1, 4):
            x_copy(f, i).wait_recv()
            total = total + xr[f, i - 1].astype(F32)
        fin[f] = total.astype(BF16)
        for i in (2, 1, 3, 0):
            fin_copy(f, i).start()

    for j in range(4):
        for side in range(2):
            x_send(side, j).wait_recv()
    x_relay().start()
    w_step(0)
    for zp in range(8):
        x_own(zp).wait()

    for h in range(2):
        remote(
            kv_all.at[c, yh], kv_oth.at[h], k1_s.at[h], k1_r.at[h], sibling
        ).wait_recv()
    for side in range(2):
        kv2(side).start()
    transpose_kv(yh)
    theirs = pl.ds(4 * (1 - c), 4)
    remote(
        xb.at[theirs, pl.ds(384, 384)], xb.at[theirs, pl.ds(384, 384)], xsib_s, xsib_r, sibling
    ).wait_recv()
    rs_step(0, 0)
    w_step(1)
    rs_step(0, 1)
    for side in range(2):
        rows = pl.ds(192 * side, 192)
        remote(
            kv_oth.at[0, rows], kv_all.at[c, 1 - yh, rows], k2_s.at[side], k2_r.at[side], sibling
        ).wait_recv()
    kv_sibling(1).start()
    transpose_kv(1 - yh)
    rs_step(1, 0)
    w_step(2)
    rs_step(0, 2)
    rs_step(1, 1)
    rs_step(0, 3)
    rs_step(1, 2)
    w_step(3)
    rs_last(0)
    rs_step(1, 3)
    x_last(0)
    rs_last(1)

    for i in range(2):
        ref = kv_all.at[1 - c, yh] if i == 0 else kv_all.at[1 - c, 1 - yh]
        remote(ref, ref, ks_s.at[i], ks_r.at[i], sibling).wait_recv()

    def w_ready(j):
        pltpu.make_async_copy(wz.at[0], wfull.at[j, c, :, rows_p], wloc.at[j]).wait()
        remote(
            wz.at[0], wfull.at[j, 1 - c, :, rows_p], wsib_s.at[0], wsib_r.at[j], sibling
        ).wait_recv()
        rows_o = pl.ds(pl.multiple_of((1 - p) * 256, 256), 256)
        for cc in range(2):
            for side in range(2):
                remote(
                    wz.at[0, side], wfull.at[j, cc, side, rows_o],
                    wx_s.at[0, side], wx_r.at[j, cc, side], sibling,
                ).wait_recv()

    def ig_step(j):
        w_ready(j)
        total = None
        for cc in range(2):
            for h in range(2):
                term = dot(kv_all[cc, h], wfull[j, cc, h], ((1,), (1,)))
                total = term if total is None else total + term
        ig[:, 512 * j:512 * j + 512] = total.astype(BF16)

    ig_step(0)
    ig_step(1)
    x_last(1)
    ig_step(2)
    ig_step(3)

    for hs in range(2):
        for xx in range(4):
            remote(
                fin.at[0], wgt.at[hs, pl.ds(64 * xx, 64)], fin_s.at[0, 0], fin_r.at[hs, xx], sibling
            ).wait_recv()
        wg[256 * hs:256 * hs + 256, :] = wgt[hs].astype(F32).T

    for i in range(2):
        @pl.when(2 * yl + i != y)
        def _():
            w0_remote(i).wait_send()
    for side in range(2):
        for j in range(4):
            x_send(side, j).wait_send()
        kv1(side).wait_send()
        kv2(side).wait_send()
        kv_sibling(side).wait_send()
        for s in range(4):
            wz_copy(side, s).wait_send()
            for f in range(2):
                rs_copy(f, side, s).wait_send()
    x_relay().wait_send()
    for zp in range(8):
        for side in range(2):
            spread_x(zp, side).wait_send()

        @pl.when(zp // 4 != c)
        def _():
            spread_sibling(zp).wait_send()
    for f in range(2):
        for i in range(1, 4):
            x_copy(f, i).wait_send()
        for i in range(4):
            fin_copy(f, i).wait_send()


def shards(layer_input, queries, keys, values, kv_weight, out_grad, doc_lengths):
    vmem = pl.BlockSpec(memory_space=pltpu.VMEM)
    hbm = pl.BlockSpec(memory_space=pl.ANY)
    smem = pl.BlockSpec(memory_space=pltpu.SMEM)
    dma = pltpu.SemaphoreType.DMA
    return pl.pallas_call(
        kernel,
        out_shape=(
            jax.ShapeDtypeStruct((384, 2048), BF16),
            jax.ShapeDtypeStruct((384, 1024), BF16),
            jax.ShapeDtypeStruct((512, 256), F32),
        ),
        in_specs=[hbm, vmem, vmem, vmem, vmem, vmem, smem],
        out_specs=(vmem, vmem, vmem),
        scratch_shapes=[
            pltpu.VMEM((8, 768, 256), BF16),
            pltpu.VMEM((8, 2, 256, 256), BF16),
            pltpu.VMEM((4, 2, 2, 512, 256), BF16),
            pltpu.VMEM((2, 2, 384, 256), BF16),
            pltpu.VMEM((2, 384, 256), BF16),
            pltpu.VMEM((2, 256, 768), BF16),
            pltpu.VMEM((2, 2, 4, 256, 256), BF16),
            pltpu.VMEM((2, 2, 4, 256, 256), BF16),
            pltpu.VMEM((2, 256, 256), F32),
            pltpu.VMEM((2, 256, 256), BF16),
            pltpu.VMEM((2, 3, 64, 256), BF16),
            pltpu.VMEM((2, 64, 256), BF16),
            pltpu.VMEM((2, 256, 256), BF16),
            pltpu.VMEM((384, 384), F32),
            pltpu.VMEM((384, 128), F32),
            pltpu.VMEM((384, 128), F32),
            dma((8,)), dma((2, 4)), dma((2, 4)), dma, dma,
            dma((2,)), dma((2,)), dma((2, 4)), dma((2, 4)),
            dma((8, 2)), dma((4, 2, 2)), dma((8,)), dma((4,)), dma((4,)),
            dma((2,)), dma((2,)), dma((2,)), dma((2,)), dma((2,)), dma((2,)),
            dma((2, 2, 4)), dma((2, 2, 4)), dma((2, 3)), dma((2, 3)),
            dma((2, 4)), dma((2, 4)),
        ],
        compiler_params=pltpu.CompilerParams(
            collective_id=0, has_side_effects=True, vmem_limit_bytes=56 << 20
        ),
        cost_estimate=pl.CostEstimate(
            flops=5 * 10**9, bytes_accessed=2 * 10**7, transcendentals=10**6
        ),
        name="kv_back",
    )(layer_input, queries, keys, values, kv_weight, out_grad, doc_lengths)


def solution(mesh):
    placed = (
        P(("blk", "dp"), None),
        P(("blk", "dp"), "tp"),
        P(("blk", "dp"), "tp"),
        P(("blk", "dp"), "tp"),
        P("blk", "tp"),
        P(("blk", "dp"), "tp"),
        P(("blk", "dp"), None),
    )
    return jax.shard_map(
        shards,
        mesh=mesh,
        in_specs=placed,
        out_specs=(P(("blk", "dp"), "tp"), P(("blk", "dp"), "tp"), P("blk", "tp")),
        check_vma=False,
    )
```

```python
import functools

import jax
import jax.numpy as jnp
from jax import lax
from jax.experimental import pallas as pl
from jax.experimental.pallas import tpu as pltpu
from jax.sharding import PartitionSpec as P

HD = 128
BY_USE = (4, 3, 5, 2, 6, 1, 7, 0)
MESH = pl.DeviceIdType.MESH
F32 = jnp.float32
BF16 = jnp.bfloat16


def device(x, y, z, c):
    return {"blk": (y % 2) * 8 + z, "tp": (y // 2) * 2 + c, "dp": x}


def dot(a, b, dims):
    return lax.dot_general(a, b, (dims, ((), ())), preferred_element_type=F32)


def kernel(
    li, q_in, k_in, v_in, w, do_in, dl,
    ig, qg, wg,
    q, k, v, do, xb, wz, wfull, kv_all, kv_oth, kvt, sbuf, rbuf, facc, xs, xr, fin, wgt,
    igo, igi, bias, kacc, vacc,
    in_sem, xo_sem, xs_s, xs_r, xsib_s, xsib_r,
    w0_s, w0_r, wz_s, wz_r, wx_s, wx_r, wsib_s, wsib_r, wloc,
    k1_s, k1_r, k2_s, k2_r, ks_s, ks_r, ko_s, ko_r,
    rs_s, rs_r, xr_s, xr_r, fin_s, fin_r, ig_s, ig_r,
):
    blk, tp, x = lax.axis_index("blk"), lax.axis_index("tp"), lax.axis_index("dp")
    yl, z, yh, c = blk // 8, blk % 8, tp // 2, tp % 2
    y = yh * 2 + yl
    p = x % 2

    def remote(src, dst, ssem, rsem, dev):
        return pltpu.make_async_remote_copy(
            src_ref=src, dst_ref=dst, send_sem=ssem, recv_sem=rsem,
            device_id=dev, device_id_type=MESH,
        )

    def at(dx=0, dy=0, dz=0, core=None):
        return device((x + dx) % 4, (y + dy) % 4, (z + dz) % 8, c if core is None else core)

    sibling = at(core=1 - c)

    partners = [at(dz=1), at(dz=7), sibling, at(dy=1), at(dy=2), at(dy=3), at(dx=2)]
    for dx in (1, 3):
        for core in (0, 1):
            partners.append(at(dx=dx, core=core))
    for dx in (1, 2, 3):
        for dy in (1, 3):
            partners.append(at(dx=dx, dy=dy))
    barrier = pltpu.get_barrier_semaphore()
    for d in partners:
        pl.semaphore_signal(barrier, inc=1, device_id=d, device_id_type=MESH)

    def x_own(zp):
        cols = pl.ds(pl.multiple_of(((1 - yl) * 8 + zp) * 512 + yh * 256, 256), 256)
        return pltpu.make_async_copy(li.at[:, cols], xb.at[zp, pl.ds(0, 384)], xo_sem.at[zp])

    loads = [
        pltpu.make_async_copy(a, b, in_sem.at[i])
        for i, (a, b) in enumerate(((q_in, q), (k_in, k), (v_in, v), (do_in, do)))
    ]
    for load in loads:
        load.start()

    pl.semaphore_wait(barrier, len(partners))

    rows_p = pl.ds(pl.multiple_of(p * 128, 128), 128)
    rows_o = pl.ds(pl.multiple_of((1 - p) * 128, 128), 128)

    def w0_rows(i):
        return w.at[pl.ds(pl.multiple_of(256 * i + p * 128, 128), 128)]

    def w0_remote(i):
        return remote(
            w0_rows(i), wz.at[z, yh], w0_s.at[i], w0_r.at[yh],
            device(x, 2 * yl + i, z, c),
        )

    def w0_local(i):
        return pltpu.make_async_copy(w0_rows(i), wz.at[z, yh], w0_r.at[yh])

    for i in range(2):
        @pl.when(2 * yl + i != y)
        def _():
            w0_remote(i).start()

        @pl.when(2 * yl + i == y)
        def _():
            w0_local(i).start()

    def x_send(side, zp):
        ydst = (y + 1) % 4 if side == 0 else (y + 3) % 4
        cols = pl.ds(pl.multiple_of((yl * 8 + zp) * 512 + (ydst // 2) * 256, 256), 256)
        return remote(
            li.at[pl.ds(192 * side, 192), cols],
            xb.at[zp, pl.ds(384 + 192 * side, 192)],
            xs_s.at[side, zp % 4], xs_r.at[side, zp % 4], device(x, ydst, z, c),
        )

    def x_relay(zp):
        ref = xb.at[zp, pl.ds(384, 384)]
        return remote(ref, ref, xsib_s.at[zp % 4], xsib_r.at[zp % 4], sibling)

    def block(dz):
        return (z + dz) % 8

    for dz in BY_USE:
        zp = block(dz)

        @pl.when(zp // 4 == c)
        def _():
            for side in range(2):
                x_send(side, zp).start()

    for dz in BY_USE:
        x_own(block(dz)).start()

    def x_pass(dz):
        zp = block(dz)

        @pl.when(zp // 4 == c)
        def _():
            for side in range(2):
                x_send(side, zp).wait_recv()
            x_relay(zp).start()

    def x_ready(dz):
        zp = block(dz)
        x_own(zp).wait()

        @pl.when(zp // 4 != c)
        def _():
            x_relay(zp).wait_recv()

    def spread_x(zp, side):
        j, cz = zp % 4, zp // 4
        return remote(
            wz.at[zp, side], wfull.at[j, c, side, rows_p],
            wx_s.at[zp, side], wx_r.at[j, c, side],
            at(dx=1 if side == 0 else 3, core=cz),
        )

    def spread_sibling(zp):
        j = zp % 4
        return remote(
            wz.at[zp], wfull.at[j, c, :, rows_p], wsib_s.at[zp], wsib_r.at[j], sibling
        )

    def spread_local(zp):
        j = zp % 4
        return pltpu.make_async_copy(wz.at[zp], wfull.at[j, c, :, rows_p], wloc.at[j])

    def spread(zp):
        for side in range(2):
            spread_x(zp, side).start()

        @pl.when(zp // 4 == c)
        def _():
            spread_local(zp).start()

        @pl.when(zp // 4 != c)
        def _():
            spread_sibling(zp).start()

    def wz_copy(direction, s):
        zp = (z - s + 8) % 8 if direction == 0 else (z + s) % 8
        ref = wz.at[zp, direction] if s == 3 else wz.at[zp]
        return remote(
            ref, ref, wz_s.at[direction, s], wz_r.at[direction, s],
            at(dz=1 if direction == 0 else 7),
        )

    def wz_wait(direction, s):
        zp = (z - s + 7) % 8 if direction == 0 else (z + s + 1) % 8
        ref = wz.at[zp, direction] if s == 3 else wz.at[zp]
        remote(ref, ref, wz_s.at[direction, s], wz_r.at[direction, s], sibling).wait_recv()
        return zp

    def w_begin():
        for h in range(2):
            remote(w0_rows(0), wz.at[z, h], w0_s.at[h], w0_r.at[h], sibling).wait_recv()
        for direction in range(2):
            wz_copy(direction, 0).start()
        spread(z)

    def w_step(s):
        arrived = [wz_wait(direction, s) for direction in range(2)]
        if s < 3:
            for direction in range(2):
                wz_copy(direction, s + 1).start()
            for zp in arrived:
                spread(zp)
        else:
            spread(arrived[0])

    lens = [dl[0, i] for i in range(3)]
    ends = [lens[0], lens[0] + lens[1], lens[0] + lens[1] + lens[2]]

    def documents(shape, dim):
        pos = lax.broadcasted_iota(jnp.int32, shape, dim)
        return pos, sum((pos >= e).astype(jnp.int32) for e in ends)

    kpos, kdoc = documents((384, 1), 0)
    qpos, qdoc = documents((1, 384), 1)
    bias[...] = jnp.where((kdoc == qdoc) & (kpos <= qpos), 0.0, -1e30).astype(F32)
    kacc[...] = jnp.zeros_like(kacc)
    vacc[...] = jnp.zeros_like(vacc)
    scale = 1.0 / HD**0.5

    def head(h, carry):
        lanes = pl.ds(pl.multiple_of(h * HD, HD), HD)
        for b in range(3):
            n = 128 * (b + 1)
            rows = pl.ds(128 * b, 128)
            qb, gb = q[rows, lanes], do[rows, lanes]
            s = dot(k[:n], qb, ((1,), (1,))) + bias[:n, 128 * b:n]
            e = jnp.exp((s - jnp.max(s, axis=0, keepdims=True)) * scale)
            probs = e * (1.0 / jnp.sum(e, axis=0, keepdims=True))
            pg = dot(v[:n], gb, ((1,), (1,)))
            inner = jnp.sum(probs * pg, axis=0, keepdims=True)
            ds = (probs * (pg - inner) * scale).astype(BF16)
            qg[rows, lanes] = dot(ds, k[:n], ((0,), (0,))).astype(BF16)
            kacc[:n] += dot(ds, qb, ((1,), (0,)))
            vacc[:n] += dot(probs.astype(BF16), gb, ((1,), (0,)))
        return carry

    for load in loads:
        load.wait()
    lax.fori_loop(0, 2, head, 0)
    w_begin()
    lax.fori_loop(2, 5, head, 0)
    for dz in BY_USE[:3]:
        x_pass(dz)
    lax.fori_loop(5, 8, head, 0)

    kv_all[c, yh, :, :HD] = kacc[...].astype(BF16)
    kv_all[c, yh, :, HD:] = vacc[...].astype(BF16)

    def kv1(side):
        return remote(
            kv_all.at[c, yh], kv_oth.at[c, yh], k1_s.at[side], k1_r.at[yh],
            at(dy=1 if side == 0 else 3),
        )

    for side in range(2):
        kv1(side).start()

    def kv_sibling(i):
        ref = kv_all.at[c, yh] if i == 0 else kv_all.at[c, 1 - yh]
        return remote(ref, ref, ks_s.at[i], ks_r.at[i], sibling)

    kv_sibling(0).start()

    def kv2(side):
        hsrc = ((y + 3) % 4) // 2 if side == 0 else ((y + 1) % 4) // 2
        rows = pl.ds(192 * side, 192)
        return remote(
            kv_oth.at[c, hsrc, rows], kv_all.at[c, hsrc, rows], k2_s.at[side], k2_r.at[side],
            at(dy=1 if side == 0 else 3),
        )

    def transpose_kv(h):
        kvt[h, :, :384] = kv_all[c, h].astype(F32).T.astype(BF16)
        kvt[h, :, 384:] = kv_oth[c, h].astype(F32).T.astype(BF16)

    def partial(f, zp, first=0, count=128):
        h = yh if f < 2 else 1 - yh
        first += 128 * (f % 2)
        return dot(kvt[h, first:first + count, :], xb[zp], ((1,), (0,)))

    def rs_copy(f, direction, s):
        half = pl.ds(0, 64) if s == 0 else pl.ds(0, 128)
        return remote(
            sbuf.at[f, direction, s, half], rbuf.at[f, direction, s, half],
            rs_s.at[f, direction, s], rs_r.at[f, direction, s],
            at(dz=1 if direction == 0 else 7),
        )

    def rs_step(f, s):
        terms = []
        for direction in range(2):
            zd = (z + 4 - s) % 8 if direction == 0 else (z + 4 + s) % 8
            if s == 0:
                terms.append(partial(f, zd, 64 * direction, 64))
            else:
                terms.append(partial(f, zd))
        for direction in range(2):
            term = terms[direction]
            if s == 0:
                sbuf[f, direction, 0, :64] = term.astype(BF16)
            else:
                rs_copy(f, direction, s - 1).wait_recv()
                if s == 1:
                    mine = slice(64 * direction, 64 * direction + 64)
                    rest = slice(64 - 64 * direction, 128 - 64 * direction)
                    sbuf[f, direction, 1, rest] = term[rest].astype(BF16)
                    sbuf[f, direction, 1, mine] = (
                        term[mine] + rbuf[f, direction, 0, :64].astype(F32)
                    ).astype(BF16)
                else:
                    sbuf[f, direction, s] = (
                        term + rbuf[f, direction, s - 1].astype(F32)
                    ).astype(BF16)
            rs_copy(f, direction, s).start()

    def rs_last(f):
        total = partial(f, z)
        for direction in range(2):
            rs_copy(f, direction, 3).wait_recv()
            total = total + rbuf[f, direction, 3].astype(F32)
        half = slice(128 * (f % 2), 128 * (f % 2) + 128)
        facc[f // 2, half] = total
        xs[f // 2, half] = total.astype(BF16)

    def x_copy(i, n):
        quarter = pl.ds(pl.multiple_of(((x + n) % 4) * 64, 64), 64)
        return remote(
            xs.at[i, quarter], xr.at[i, n - 1], xr_s.at[i, n - 1], xr_r.at[i, n - 1], at(dx=n)
        )

    def x_first(i):
        for n in (2, 1, 3):
            x_copy(i, n).start()

    def fin_copy(i, n):
        h = yh if i == 0 else 1 - yh
        cols = pl.ds(pl.multiple_of(x * 64, 64), 64)
        return remote(
            fin.at[i], wgt.at[yh, cols], fin_s.at[i, n], fin_r.at[yh, x],
            device((x + n) % 4, 2 * h + 1 - yl, z, c),
        )

    def x_last(i):
        total = facc[i, pl.ds(pl.multiple_of(x * 64, 64), 64)]
        for n in range(1, 4):
            x_copy(i, n).wait_recv()
            total = total + xr[i, n - 1].astype(F32)
        fin[i] = total.astype(BF16)
        for n in (2, 1, 3, 0):
            fin_copy(i, n).start()

    def w_ready(j):
        pltpu.make_async_copy(wz.at[0], wfull.at[j, c, :, rows_p], wloc.at[j]).wait()
        remote(
            wz.at[0], wfull.at[j, 1 - c, :, rows_p], wsib_s.at[0], wsib_r.at[j], sibling
        ).wait_recv()
        for cc in range(2):
            for side in range(2):
                remote(
                    wz.at[0, side], wfull.at[j, cc, side, rows_o],
                    wx_s.at[0, side], wx_r.at[j, cc, side], sibling,
                ).wait_recv()

    def ig_copy(j):
        return remote(
            igo.at[j], igi.at[j], ig_s.at[j], ig_r.at[j], device(x, 2 * yh + 1 - yl, z, c)
        )

    def ig_step(j):
        w_ready(j)

        def rows_of(kv):
            total = None
            for cc in range(2):
                for h in range(2):
                    term = dot(kv[cc, h], wfull[j, cc, h], ((1,), (1,)))
                    total = term if total is None else total + term
            return total.astype(BF16)

        igo[j] = rows_of(kv_oth)
        ig_copy(j).start()
        ig[:, pl.ds(pl.multiple_of(512 * j + 256 * yl, 256), 256)] = rows_of(kv_all)

    def ig_last(j):
        ig_copy(j).wait_recv()
        ig[:, pl.ds(pl.multiple_of(512 * j + 256 * (1 - yl), 256), 256)] = igi[j]

    def kv_own_sibling(i):
        ref = kv_all.at[1 - c, yh] if i == 0 else kv_all.at[1 - c, 1 - yh]
        remote(ref, ref, ks_s.at[i], ks_r.at[i], sibling).wait_recv()

    def kv_other(core):
        return remote(kv_oth.at[core], kv_oth.at[core], ko_s, ko_r, sibling)

    for dz in BY_USE[3:]:
        x_pass(dz)
    w_step(0)
    w_step(1)
    for h in range(2):
        remote(
            kv_all.at[c, yh], kv_oth.at[c, h], k1_s.at[h], k1_r.at[h], sibling
        ).wait_recv()
    for side in range(2):
        kv2(side).start()
    kv_other(c).start()
    transpose_kv(yh)
    x_ready(4)
    rs_step(0, 0)
    rs_step(1, 0)
    w_step(2)
    x_ready(3)
    x_ready(5)
    rs_step(0, 1)
    rs_step(1, 1)
    for side in range(2):
        rows = pl.ds(192 * side, 192)
        remote(
            kv_oth.at[c, 0, rows], kv_all.at[c, 1 - yh, rows], k2_s.at[side], k2_r.at[side],
            sibling,
        ).wait_recv()
    kv_sibling(1).start()
    transpose_kv(1 - yh)
    rs_step(2, 0)
    rs_step(3, 0)
    x_ready(2)
    x_ready(6)
    rs_step(0, 2)
    rs_step(1, 2)
    w_step(3)
    rs_step(2, 1)
    rs_step(3, 1)
    for i in range(2):
        kv_own_sibling(i)
    kv_other(1 - c).wait_recv()
    ig_step(0)
    x_ready(1)
    x_ready(7)
    rs_step(0, 3)
    rs_step(1, 3)
    ig_step(1)
    rs_step(2, 2)
    rs_step(3, 2)
    ig_step(2)
    x_ready(0)
    rs_last(0)
    rs_last(1)
    x_first(0)
    ig_step(3)
    rs_step(2, 3)
    rs_step(3, 3)
    x_last(0)
    rs_last(2)
    rs_last(3)
    x_first(1)
    for j in range(3):
        ig_last(j)
    x_last(1)
    ig_last(3)

    for hs in range(2):
        for xx in range(4):
            remote(
                fin.at[0], wgt.at[hs, pl.ds(64 * xx, 64)], fin_s.at[0, 0], fin_r.at[hs, xx], sibling
            ).wait_recv()
        wg[256 * hs:256 * hs + 256, :] = wgt[hs].astype(F32).T

    for i in range(2):
        @pl.when(2 * yl + i != y)
        def _():
            w0_remote(i).wait_send()
    for side in range(2):
        kv1(side).wait_send()
        kv2(side).wait_send()
        kv_sibling(side).wait_send()
        for s in range(4):
            wz_copy(side, s).wait_send()
            for f in range(4):
                rs_copy(f, side, s).wait_send()
    kv_other(c).wait_send()
    for j in range(4):
        zp = 4 * c + j
        for side in range(2):
            x_send(side, zp).wait_send()
        x_relay(zp).wait_send()
        ig_copy(j).wait_send()
    for zp in range(8):
        for side in range(2):
            spread_x(zp, side).wait_send()

        @pl.when(zp // 4 != c)
        def _():
            spread_sibling(zp).wait_send()
    for i in range(2):
        for n in range(1, 4):
            x_copy(i, n).wait_send()
        for n in range(4):
            fin_copy(i, n).wait_send()


def shards(layer_input, queries, keys, values, kv_weight, out_grad, doc_lengths):
    vmem = pl.BlockSpec(memory_space=pltpu.VMEM)
    hbm = pl.BlockSpec(memory_space=pl.ANY)
    smem = pl.BlockSpec(memory_space=pltpu.SMEM)
    dma = pltpu.SemaphoreType.DMA
    return pl.pallas_call(
        kernel,
        out_shape=(
            jax.ShapeDtypeStruct((384, 2048), BF16),
            jax.ShapeDtypeStruct((384, 1024), BF16),
            jax.ShapeDtypeStruct((512, 256), F32),
        ),
        in_specs=[hbm, hbm, hbm, hbm, hbm, hbm, smem],
        out_specs=(vmem, vmem, vmem),
        scratch_shapes=[
            pltpu.VMEM((384, 1024), BF16),
            pltpu.VMEM((384, 128), BF16),
            pltpu.VMEM((384, 128), BF16),
            pltpu.VMEM((384, 1024), BF16),
            pltpu.VMEM((8, 768, 256), BF16),
            pltpu.VMEM((8, 2, 128, 256), BF16),
            pltpu.VMEM((4, 2, 2, 256, 256), BF16),
            pltpu.VMEM((2, 2, 384, 256), BF16),
            pltpu.VMEM((2, 2, 384, 256), BF16),
            pltpu.VMEM((2, 256, 768), BF16),
            pltpu.VMEM((4, 2, 4, 128, 256), BF16),
            pltpu.VMEM((4, 2, 4, 128, 256), BF16),
            pltpu.VMEM((2, 256, 256), F32),
            pltpu.VMEM((2, 256, 256), BF16),
            pltpu.VMEM((2, 3, 64, 256), BF16),
            pltpu.VMEM((2, 64, 256), BF16),
            pltpu.VMEM((2, 256, 256), BF16),
            pltpu.VMEM((4, 384, 256), BF16),
            pltpu.VMEM((4, 384, 256), BF16),
            pltpu.VMEM((384, 384), F32),
            pltpu.VMEM((384, 128), F32),
            pltpu.VMEM((384, 128), F32),
            dma((4,)), dma((8,)), dma((2, 4)), dma((2, 4)), dma((4,)), dma((4,)),
            dma((2,)), dma((2,)), dma((2, 4)), dma((2, 4)),
            dma((8, 2)), dma((4, 2, 2)), dma((8,)), dma((4,)), dma((4,)),
            dma((2,)), dma((2,)), dma((2,)), dma((2,)), dma((2,)), dma((2,)), dma, dma,
            dma((4, 2, 4)), dma((4, 2, 4)), dma((2, 3)), dma((2, 3)),
            dma((2, 4)), dma((2, 4)), dma((4,)), dma((4,)),
        ],
        compiler_params=pltpu.CompilerParams(
            collective_id=0, has_side_effects=True, vmem_limit_bytes=56 << 20
        ),
        cost_estimate=pl.CostEstimate(
            flops=5 * 10**9, bytes_accessed=2 * 10**7, transcendentals=10**6
        ),
        name="kv_back",
    )(layer_input, queries, keys, values, kv_weight, out_grad, doc_lengths)


def solution(mesh):
    placed = (
        P(("blk", "dp"), None),
        P(("blk", "dp"), "tp"),
        P(("blk", "dp"), "tp"),
        P(("blk", "dp"), "tp"),
        P("blk", "tp"),
        P(("blk", "dp"), "tp"),
        P(("blk", "dp"), None),
    )
    return jax.shard_map(
        shards,
        mesh=mesh,
        in_specs=placed,
        out_specs=(P(("blk", "dp"), "tp"), P(("blk", "dp"), "tp"), P("blk", "tp")),
        check_vma=False,
    )
```

```python
import functools

import jax
import jax.numpy as jnp
from jax import lax
from jax.experimental import pallas as pl
from jax.experimental.pallas import tpu as pltpu
from jax.sharding import PartitionSpec as P

HD = 128
BY_USE = (4, 3, 5, 2, 6, 1, 7, 0)
MESH = pl.DeviceIdType.MESH
F32 = jnp.float32
BF16 = jnp.bfloat16


def device(x, y, z, c):
    return {"blk": (y % 2) * 8 + z, "tp": (y // 2) * 2 + c, "dp": x}


def dot(a, b, dims):
    return lax.dot_general(a, b, (dims, ((), ())), preferred_element_type=F32)


def kernel(
    li, q_in, k_in, v_in, w, do_in, dl,
    ig_out, qg_out, wg_out,
    q, k, v, do, probs, qg, xb, wz, wfull, kv_all, kv_oth, kvt, sbuf, rbuf, facc, xs, xr, fin, wgt,
    iga, igo, igi, bias, kacc, vacc,
    in_sem, out_sem, xo_sem, xs_s, xs_r, xsib_s, xsib_r,
    w0_s, w0_r, wz_s, wz_r, wx_s, wx_r, wsib_s, wsib_r, wloc,
    k1_s, k1_r, k2_s, k2_r, ks_s, ks_r,
    rs_s, rs_r, xr_s, xr_r, fin_s, fin_r, ig_s, ig_r,
):
    blk, tp, x = lax.axis_index("blk"), lax.axis_index("tp"), lax.axis_index("dp")
    yl, z, yh, c = blk // 8, blk % 8, tp // 2, tp % 2
    y = yh * 2 + yl
    p = x % 2

    def remote(src, dst, ssem, rsem, dev):
        return pltpu.make_async_remote_copy(
            src_ref=src, dst_ref=dst, send_sem=ssem, recv_sem=rsem,
            device_id=dev, device_id_type=MESH,
        )

    def at(dx=0, dy=0, dz=0, core=None):
        return device((x + dx) % 4, (y + dy) % 4, (z + dz) % 8, c if core is None else core)

    sibling = at(core=1 - c)

    partners = [at(dz=1), at(dz=7), sibling, at(dy=1), at(dy=2), at(dy=3), at(dx=2)]
    for dx in (1, 3):
        for core in (0, 1):
            partners.append(at(dx=dx, core=core))
    for dx in (1, 2, 3):
        for dy in (1, 3):
            partners.append(at(dx=dx, dy=dy))
    barrier = pltpu.get_barrier_semaphore()
    for d in partners:
        pl.semaphore_signal(barrier, inc=1, device_id=d, device_id_type=MESH)

    def x_own(zp):
        cols = pl.ds(pl.multiple_of(((1 - yl) * 8 + zp) * 512 + yh * 256, 256), 256)
        return pltpu.make_async_copy(li.at[:, cols], xb.at[zp, pl.ds(0, 384)], xo_sem.at[zp])

    loads = [
        pltpu.make_async_copy(a, b, in_sem.at[i])
        for i, (a, b) in enumerate(((q_in, q), (k_in, k), (v_in, v), (do_in, do)))
    ]
    for load in loads:
        load.start()

    pl.semaphore_wait(barrier, len(partners))

    rows_p = pl.ds(pl.multiple_of(p * 128, 128), 128)
    rows_o = pl.ds(pl.multiple_of((1 - p) * 128, 128), 128)

    def w0_rows(i):
        return w.at[pl.ds(pl.multiple_of(256 * i + p * 128, 128), 128)]

    def w0_remote(i):
        return remote(
            w0_rows(i), wz.at[z, yh], w0_s.at[i], w0_r.at[yh],
            device(x, 2 * yl + i, z, c),
        )

    def w0_local(i):
        return pltpu.make_async_copy(w0_rows(i), wz.at[z, yh], w0_r.at[yh])

    for i in range(2):
        @pl.when(2 * yl + i != y)
        def _():
            w0_remote(i).start()

        @pl.when(2 * yl + i == y)
        def _():
            w0_local(i).start()

    def x_send(side, zp):
        ydst = (y + 1) % 4 if side == 0 else (y + 3) % 4
        cols = pl.ds(pl.multiple_of((yl * 8 + zp) * 512 + (ydst // 2) * 256, 256), 256)
        return remote(
            li.at[pl.ds(192 * side, 192), cols],
            xb.at[zp, pl.ds(384 + 192 * side, 192)],
            xs_s.at[side, zp % 4], xs_r.at[side, zp % 4], device(x, ydst, z, c),
        )

    def x_relay(zp):
        ref = xb.at[zp, pl.ds(384, 384)]
        return remote(ref, ref, xsib_s.at[zp % 4], xsib_r.at[zp % 4], sibling)

    def block(dz):
        return (z + dz) % 8

    for dz in BY_USE:
        zp = block(dz)

        @pl.when(zp // 4 == c)
        def _():
            for side in range(2):
                x_send(side, zp).start()

    for dz in BY_USE:
        x_own(block(dz)).start()

    def x_pass(dz):
        zp = block(dz)

        @pl.when(zp // 4 == c)
        def _():
            for side in range(2):
                x_send(side, zp).wait_recv()
            x_relay(zp).start()

    def x_ready(dz):
        zp = block(dz)
        x_own(zp).wait()

        @pl.when(zp // 4 != c)
        def _():
            x_relay(zp).wait_recv()

    def spread_x(zp, side):
        j, cz = zp % 4, zp // 4
        return remote(
            wz.at[zp, side], wfull.at[j, c, side, rows_p],
            wx_s.at[zp, side], wx_r.at[j, c, side],
            at(dx=1 if side == 0 else 3, core=cz),
        )

    def spread_sibling(zp):
        j = zp % 4
        return remote(
            wz.at[zp], wfull.at[j, c, :, rows_p], wsib_s.at[zp], wsib_r.at[j], sibling
        )

    def spread_local(zp):
        j = zp % 4
        return pltpu.make_async_copy(wz.at[zp], wfull.at[j, c, :, rows_p], wloc.at[j])

    def spread(zp):
        for side in range(2):
            spread_x(zp, side).start()

        @pl.when(zp // 4 == c)
        def _():
            spread_local(zp).start()

        @pl.when(zp // 4 != c)
        def _():
            spread_sibling(zp).start()

    def wz_copy(direction, s):
        zp = (z - s + 8) % 8 if direction == 0 else (z + s) % 8
        ref = wz.at[zp, direction] if s == 3 else wz.at[zp]
        return remote(
            ref, ref, wz_s.at[direction, s], wz_r.at[direction, s],
            at(dz=1 if direction == 0 else 7),
        )

    def wz_wait(direction, s):
        zp = (z - s + 7) % 8 if direction == 0 else (z + s + 1) % 8
        ref = wz.at[zp, direction] if s == 3 else wz.at[zp]
        remote(ref, ref, wz_s.at[direction, s], wz_r.at[direction, s], sibling).wait_recv()
        return zp

    def w_begin():
        for h in range(2):
            remote(w0_rows(0), wz.at[z, h], w0_s.at[h], w0_r.at[h], sibling).wait_recv()
        for direction in range(2):
            wz_copy(direction, 0).start()
        spread(z)

    def w_step(s):
        arrived = [wz_wait(direction, s) for direction in range(2)]
        if s < 3:
            for direction in range(2):
                wz_copy(direction, s + 1).start()
            for zp in arrived:
                spread(zp)
        else:
            spread(arrived[0])

    lens = [dl[0, i] for i in range(3)]
    ends = [lens[0], lens[0] + lens[1], lens[0] + lens[1] + lens[2]]

    def documents(shape, dim):
        pos = lax.broadcasted_iota(jnp.int32, shape, dim)
        return pos, sum((pos >= e).astype(jnp.int32) for e in ends)

    kpos, kdoc = documents((384, 1), 0)
    qpos, qdoc = documents((1, 384), 1)
    bias[...] = jnp.where((kdoc == qdoc) & (kpos <= qpos), 0.0, -1e30).astype(F32)
    kacc[...] = jnp.zeros_like(kacc)
    vacc[...] = jnp.zeros_like(vacc)
    scale = 1.0 / HD**0.5

    def value_head(h, carry):
        lanes = pl.ds(pl.multiple_of(h * HD, HD), HD)
        for b in range(3):
            n = 128 * (b + 1)
            rows = pl.ds(128 * b, 128)
            s = dot(k[:n], q[rows, lanes], ((1,), (1,))) + bias[:n, 128 * b:n]
            e = jnp.exp((s - jnp.max(s, axis=0, keepdims=True)) * scale)
            soft = e * (1.0 / jnp.sum(e, axis=0, keepdims=True))
            probs[h, :n, 128 * b:n] = soft
            vacc[:n] += dot(soft.astype(BF16), do[rows, lanes], ((1,), (0,)))
        return carry

    def key_head(h, carry):
        lanes = pl.ds(pl.multiple_of(h * HD, HD), HD)
        for b in range(3):
            n = 128 * (b + 1)
            rows = pl.ds(128 * b, 128)
            soft = probs[h, :n, 128 * b:n]
            pg = dot(v[:n], do[rows, lanes], ((1,), (1,)))
            inner = jnp.sum(soft * pg, axis=0, keepdims=True)
            ds = (soft * (pg - inner) * scale).astype(BF16)
            qg[rows, lanes] = dot(ds, k[:n], ((0,), (0,))).astype(BF16)
            kacc[:n] += dot(ds, q[rows, lanes], ((1,), (0,)))
        return carry

    def part(i):
        return pl.ds(128 * (1 - i), 128)

    def kv1(i, side):
        return remote(
            kv_all.at[c, yh, :, part(i)], kv_oth.at[c, yh, :, part(i)],
            k1_s.at[i, side], k1_r.at[i, yh], at(dy=1 if side == 0 else 3),
        )

    def kv1_start(i, acc):
        kv_all[c, yh, :, part(i)] = acc[...].astype(BF16)
        for side in range(2):
            kv1(i, side).start()

    def kv2(i, side):
        hsrc = ((y + 3) % 4) // 2 if side == 0 else ((y + 1) % 4) // 2
        rows = pl.ds(192 * side, 192)
        return remote(
            kv_oth.at[c, hsrc, rows, part(i)], kv_all.at[c, hsrc, rows, part(i)],
            k2_s.at[i, side], k2_r.at[i, side], at(dy=1 if side == 0 else 3),
        )

    def transpose_kv(i, h):
        kvt[h, part(i), :384] = kv_all[c, h, :, part(i)].astype(F32).T.astype(BF16)
        kvt[h, part(i), 384:] = kv_oth[c, h, :, part(i)].astype(F32).T.astype(BF16)

    def kv1_ready(i):
        for h in range(2):
            remote(
                kv_oth.at[c, h, :, part(i)], kv_oth.at[c, h, :, part(i)],
                k1_s.at[i, h], k1_r.at[i, h], sibling,
            ).wait_recv()
        for side in range(2):
            kv2(i, side).start()
        transpose_kv(i, yh)

    def kv2_ready(i):
        for side in range(2):
            rows = pl.ds(192 * side, 192)
            ref = kv_all.at[c, 1 - yh, rows, part(i)]
            remote(ref, ref, k2_s.at[i, side], k2_r.at[i, side], sibling).wait_recv()
        transpose_kv(i, 1 - yh)

    def kv_sibling(i, core):
        ref = (kv_all.at[core, yh], kv_all.at[core, 1 - yh], kv_oth.at[core])[i]
        return remote(ref, ref, ks_s.at[i], ks_r.at[i], sibling)

    def partial(f, zp, first=0, count=128):
        h = yh if f % 2 == 0 else 1 - yh
        first += 128 * (1 - f // 2)
        return dot(kvt[h, first:first + count, :], xb[zp], ((1,), (0,)))

    def rs_copy(f, direction, s):
        half = pl.ds(0, 64) if s == 0 else pl.ds(0, 128)
        return remote(
            sbuf.at[f, direction, s, half], rbuf.at[f, direction, s, half],
            rs_s.at[f, direction, s], rs_r.at[f, direction, s],
            at(dz=1 if direction == 0 else 7),
        )

    def rs_step(f, s):
        terms = []
        for direction in range(2):
            zd = (z + 4 - s) % 8 if direction == 0 else (z + 4 + s) % 8
            if s == 0:
                terms.append(partial(f, zd, 64 * direction, 64))
            else:
                terms.append(partial(f, zd))
        for direction in range(2):
            term = terms[direction]
            if s == 0:
                sbuf[f, direction, 0, :64] = term.astype(BF16)
            else:
                rs_copy(f, direction, s - 1).wait_recv()
                if s == 1:
                    mine = slice(64 * direction, 64 * direction + 64)
                    rest = slice(64 - 64 * direction, 128 - 64 * direction)
                    sbuf[f, direction, 1, rest] = term[rest].astype(BF16)
                    sbuf[f, direction, 1, mine] = (
                        term[mine] + rbuf[f, direction, 0, :64].astype(F32)
                    ).astype(BF16)
                else:
                    sbuf[f, direction, s] = (
                        term + rbuf[f, direction, s - 1].astype(F32)
                    ).astype(BF16)
            rs_copy(f, direction, s).start()

    def rs_last(f):
        total = partial(f, z)
        for direction in range(2):
            rs_copy(f, direction, 3).wait_recv()
            total = total + rbuf[f, direction, 3].astype(F32)
        facc[f // 2, f % 2] = total
        xs[f // 2, f % 2] = total.astype(BF16)

    def x_copy(i, n):
        quarter = pl.ds(pl.multiple_of(((x + n) % 4) * 32, 32), 32)
        return remote(
            xs.at[i, :, quarter], xr.at[i, n - 1], xr_s.at[i, n - 1], xr_r.at[i, n - 1],
            at(dx=n),
        )

    def x_first(i):
        for n in (2, 1, 3):
            x_copy(i, n).start()

    def fin_copy(i, slot, n):
        h = yh if slot == 0 else 1 - yh
        cols = pl.ds(pl.multiple_of(128 * (1 - i) + x * 32, 32), 32)
        return remote(
            fin.at[i, slot], wgt.at[yh, cols], fin_s.at[i, slot, n], fin_r.at[i, yh, x],
            device((x + n) % 4, 2 * h + 1 - yl, z, c),
        )

    def x_last(i):
        total = facc[i, :, pl.ds(pl.multiple_of(x * 32, 32), 32)]
        for n in range(1, 4):
            x_copy(i, n).wait_recv()
            total = total + xr[i, n - 1].astype(F32)
        fin[i] = total.astype(BF16)
        for n in (2, 1, 3, 0):
            for slot in range(2):
                fin_copy(i, slot, n).start()

    def w_ready(j):
        pltpu.make_async_copy(wz.at[0], wfull.at[j, c, :, rows_p], wloc.at[j]).wait()
        remote(
            wz.at[0], wfull.at[j, 1 - c, :, rows_p], wsib_s.at[0], wsib_r.at[j], sibling
        ).wait_recv()
        for cc in range(2):
            for side in range(2):
                remote(
                    wz.at[0, side], wfull.at[j, cc, side, rows_o],
                    wx_s.at[0, side], wx_r.at[j, cc, side], sibling,
                ).wait_recv()

    def ig_copy(j):
        return remote(
            igo.at[j], igi.at[j], ig_s.at[j], ig_r.at[j], device(x, 2 * yh + 1 - yl, z, c)
        )

    def ig_step(j):
        w_ready(j)

        def rows_of(kv):
            total = None
            for cc in range(2):
                for h in range(2):
                    term = dot(kv[cc, h], wfull[j, cc, h], ((1,), (1,)))
                    total = term if total is None else total + term
            return total.astype(BF16)

        igo[j] = rows_of(kv_oth)
        ig_copy(j).start()
        iga[j] = rows_of(kv_all)
        ig_store(j, 0).start()

    def ig_store(j, other):
        half = yl if other == 0 else 1 - yl
        cols = pl.ds(pl.multiple_of(512 * j + 256 * half, 256), 256)
        src = iga.at[j] if other == 0 else igi.at[j]
        return pltpu.make_async_copy(src, ig_out.at[:, cols], out_sem.at[2 * j + other])

    def ig_last(j):
        ig_copy(j).wait_recv()
        ig_store(j, 1).start()

    qg_store = pltpu.make_async_copy(qg, qg_out, out_sem.at[8])
    wg_store = pltpu.make_async_copy(wgt, wg_out, out_sem.at[9])

    for load in loads:
        load.wait()
    lax.fori_loop(0, 2, value_head, 0)
    w_begin()
    lax.fori_loop(2, 8, value_head, 0)
    kv1_start(0, vacc)
    lax.fori_loop(0, 2, key_head, 0)
    for dz in BY_USE[:3]:
        x_pass(dz)
    w_step(0)
    lax.fori_loop(2, 5, key_head, 0)
    kv1_ready(0)
    x_ready(4)
    rs_step(0, 0)
    lax.fori_loop(5, 8, key_head, 0)
    kv1_start(1, kacc)
    qg_store.start()
    kv_sibling(0, c).start()
    for dz in BY_USE[3:]:
        x_pass(dz)
    w_step(1)
    x_ready(3)
    x_ready(5)
    rs_step(0, 1)
    kv2_ready(0)
    rs_step(1, 0)
    kv1_ready(1)
    kv_sibling(2, c).start()
    rs_step(2, 0)
    x_ready(2)
    x_ready(6)
    w_step(2)
    rs_step(0, 2)
    rs_step(1, 1)
    kv2_ready(1)
    kv_sibling(1, c).start()
    rs_step(3, 0)
    rs_step(2, 1)
    x_ready(1)
    x_ready(7)
    rs_step(0, 3)
    w_step(3)
    rs_step(1, 2)
    rs_step(3, 1)
    rs_step(2, 2)
    x_ready(0)
    rs_last(0)
    for i in range(3):
        kv_sibling(i, 1 - c).wait_recv()
    ig_step(0)
    rs_step(1, 3)
    rs_step(3, 2)
    ig_step(1)
    rs_step(2, 3)
    rs_last(1)
    x_first(0)
    ig_step(2)
    rs_step(3, 3)
    rs_last(2)
    ig_step(3)
    x_last(0)
    rs_last(3)
    x_first(1)
    for j in range(3):
        ig_last(j)
    x_last(1)
    ig_last(3)

    for i in range(2):
        for hs in range(2):
            for xx in range(4):
                cols = pl.ds(128 * (1 - i) + 32 * xx, 32)
                remote(
                    fin.at[0, 0], wgt.at[hs, cols], fin_s.at[0, 0, 0], fin_r.at[i, hs, xx], sibling
                ).wait_recv()
    wg_store.start()

    for i in range(2):
        @pl.when(2 * yl + i != y)
        def _():
            w0_remote(i).wait_send()
    for side in range(2):
        for i in range(2):
            kv1(i, side).wait_send()
            kv2(i, side).wait_send()
        for s in range(4):
            wz_copy(side, s).wait_send()
            for f in range(4):
                rs_copy(f, side, s).wait_send()
    for i in range(3):
        kv_sibling(i, c).wait_send()
    for j in range(4):
        zp = 4 * c + j
        for side in range(2):
            x_send(side, zp).wait_send()
        x_relay(zp).wait_send()
        ig_copy(j).wait_send()
        for other in range(2):
            ig_store(j, other).wait()
    for zp in range(8):
        for side in range(2):
            spread_x(zp, side).wait_send()

        @pl.when(zp // 4 != c)
        def _():
            spread_sibling(zp).wait_send()
    for i in range(2):
        for n in range(1, 4):
            x_copy(i, n).wait_send()
        for slot in range(2):
            for n in range(4):
                fin_copy(i, slot, n).wait_send()
    qg_store.wait()
    wg_store.wait()


def finish(ig_in, qg_in, wgt_in, ig, qg, wg, igv, qgv, wgt, wgf, load, store):
    pieces = [
        (ig_in.at[pl.ds(96 * i, 96)], igv.at[pl.ds(96 * i, 96)], ig.at[pl.ds(96 * i, 96)])
        for i in range(4)
    ] + [
        (qg_in.at[pl.ds(192 * i, 192)], qgv.at[pl.ds(192 * i, 192)], qg.at[pl.ds(192 * i, 192)])
        for i in range(2)
    ]
    first = pltpu.make_async_copy(wgt_in, wgt, load.at[6])
    first.start()
    loads = [pltpu.make_async_copy(a, b, load.at[i]) for i, (a, b, _) in enumerate(pieces)]
    stores = [pltpu.make_async_copy(b, o, store.at[i]) for i, (_, b, o) in enumerate(pieces)]
    for copy in loads:
        copy.start()
    first.wait()
    for hs in range(2):
        wgf[256 * hs:256 * hs + 256, :] = wgt[hs].astype(F32).T
    last = pltpu.make_async_copy(wgf, wg, store.at[6])
    last.start()
    for a, b in zip(loads, stores):
        a.wait()
        b.start()
    for copy in stores:
        copy.wait()
    last.wait()


def shards(layer_input, queries, keys, values, kv_weight, out_grad, doc_lengths):
    hbm = pl.BlockSpec(memory_space=pl.ANY)
    smem = pl.BlockSpec(memory_space=pltpu.SMEM)
    dma = pltpu.SemaphoreType.DMA
    results = pl.pallas_call(
        kernel,
        out_shape=(
            jax.ShapeDtypeStruct((384, 2048), BF16),
            jax.ShapeDtypeStruct((384, 1024), BF16),
            jax.ShapeDtypeStruct((2, 256, 256), BF16),
        ),
        in_specs=[hbm, hbm, hbm, hbm, hbm, hbm, smem],
        out_specs=(hbm, hbm, hbm),
        scratch_shapes=[
            pltpu.VMEM((384, 1024), BF16),
            pltpu.VMEM((384, 128), BF16),
            pltpu.VMEM((384, 128), BF16),
            pltpu.VMEM((384, 1024), BF16),
            pltpu.VMEM((8, 384, 384), F32),
            pltpu.VMEM((384, 1024), BF16),
            pltpu.VMEM((8, 768, 256), BF16),
            pltpu.VMEM((8, 2, 128, 256), BF16),
            pltpu.VMEM((4, 2, 2, 256, 256), BF16),
            pltpu.VMEM((2, 2, 384, 256), BF16),
            pltpu.VMEM((2, 2, 384, 256), BF16),
            pltpu.VMEM((2, 256, 768), BF16),
            pltpu.VMEM((4, 2, 4, 128, 256), BF16),
            pltpu.VMEM((4, 2, 4, 128, 256), BF16),
            pltpu.VMEM((2, 2, 128, 256), F32),
            pltpu.VMEM((2, 2, 128, 256), BF16),
            pltpu.VMEM((2, 3, 2, 32, 256), BF16),
            pltpu.VMEM((2, 2, 32, 256), BF16),
            pltpu.VMEM((2, 256, 256), BF16),
            pltpu.VMEM((4, 384, 256), BF16),
            pltpu.VMEM((4, 384, 256), BF16),
            pltpu.VMEM((4, 384, 256), BF16),
            pltpu.VMEM((384, 384), F32),
            pltpu.VMEM((384, 128), F32),
            pltpu.VMEM((384, 128), F32),
            dma((4,)), dma((10,)), dma((8,)), dma((2, 4)), dma((2, 4)), dma((4,)), dma((4,)),
            dma((2,)), dma((2,)), dma((2, 4)), dma((2, 4)),
            dma((8, 2)), dma((4, 2, 2)), dma((8,)), dma((4,)), dma((4,)),
            dma((2, 2)), dma((2, 2)), dma((2, 2)), dma((2, 2)), dma((3,)), dma((3,)),
            dma((4, 2, 4)), dma((4, 2, 4)), dma((2, 3)), dma((2, 3)),
            dma((2, 2, 4)), dma((2, 2, 4)), dma((4,)), dma((4,)),
        ],
        compiler_params=pltpu.CompilerParams(
            collective_id=0, has_side_effects=True, vmem_limit_bytes=56 << 20
        ),
        cost_estimate=pl.CostEstimate(
            flops=5 * 10**9, bytes_accessed=2 * 10**7, transcendentals=10**6
        ),
        name="kv_back",
    )(layer_input, queries, keys, values, kv_weight, out_grad, doc_lengths)
    return pl.pallas_call(
        finish,
        out_shape=(
            jax.ShapeDtypeStruct((384, 2048), BF16),
            jax.ShapeDtypeStruct((384, 1024), BF16),
            jax.ShapeDtypeStruct((512, 256), F32),
        ),
        in_specs=[hbm, hbm, hbm],
        out_specs=(hbm, hbm, hbm),
        scratch_shapes=[
            pltpu.VMEM((384, 2048), BF16), pltpu.VMEM((384, 1024), BF16),
            pltpu.VMEM((2, 256, 256), BF16), pltpu.VMEM((512, 256), F32), dma((7,)), dma((7,)),
        ],
        compiler_params=pltpu.CompilerParams(vmem_limit_bytes=60 << 20),
        name="finish",
    )(*results)


def solution(mesh):
    placed = (
        P(("blk", "dp"), None),
        P(("blk", "dp"), "tp"),
        P(("blk", "dp"), "tp"),
        P(("blk", "dp"), "tp"),
        P("blk", "tp"),
        P(("blk", "dp"), "tp"),
        P(("blk", "dp"), None),
    )
    return jax.shard_map(
        shards,
        mesh=mesh,
        in_specs=placed,
        out_specs=(P(("blk", "dp"), "tp"), P(("blk", "dp"), "tp"), P("blk", "tp")),
        check_vma=False,
    )
```

```python
import functools

import jax
import jax.numpy as jnp
from jax import lax
from jax.experimental import pallas as pl
from jax.experimental.pallas import tpu as pltpu
from jax.sharding import PartitionSpec as P

HD = 128
HEADS = 8
BY_USE = (4, 3, 5, 2, 6, 1, 7, 0)
MESH = pl.DeviceIdType.MESH
F32 = jnp.float32
BF16 = jnp.bfloat16


def device(x, y, z, c):
    return {"blk": (y % 2) * 8 + z, "tp": (y // 2) * 2 + c, "dp": x}


def dot(a, b, dims):
    return lax.dot_general(a, b, (dims, ((), ())), preferred_element_type=F32)


def kernel(
    li, q_in, k_in, v_in, w, do_in, dl,
    ig_out, qg_out, wg_out,
    q, k, v, do, probs, qg, xb, wz, wfull, kv_all, kv_oth, kvt, sbuf, rbuf, facc, xs, xr, fin, wgt,
    iga, igo, igi, pt, bias, kacc, vacc,
    in_sem, out_sem, xo_sem, xs_s, xs_r, xsib_s, xsib_r,
    w0_s, w0_r, wz_s, wz_r, wx_s, wx_r, wsib_s, wsib_r, wloc,
    k1_s, k1_r, k2_s, k2_r, ks_s, ks_r,
    rs_s, rs_r, xr_s, xr_r, fin_s, fin_r, ig_s, ig_r,
):
    blk, tp, x = lax.axis_index("blk"), lax.axis_index("tp"), lax.axis_index("dp")
    yl, z, yh, c = blk // 8, blk % 8, tp // 2, tp % 2
    y = yh * 2 + yl
    p = x % 2

    def remote(src, dst, ssem, rsem, dev):
        return pltpu.make_async_remote_copy(
            src_ref=src, dst_ref=dst, send_sem=ssem, recv_sem=rsem,
            device_id=dev, device_id_type=MESH,
        )

    def at(dx=0, dy=0, dz=0, core=None):
        return device((x + dx) % 4, (y + dy) % 4, (z + dz) % 8, c if core is None else core)

    sibling = at(core=1 - c)

    partners = [at(dz=1), at(dz=7), sibling, at(dy=1), at(dy=2), at(dy=3), at(dx=2)]
    for dx in (1, 3):
        for core in (0, 1):
            partners.append(at(dx=dx, core=core))
    for dx in (1, 2, 3):
        for dy in (1, 3):
            partners.append(at(dx=dx, dy=dy))
    barrier = pltpu.get_barrier_semaphore()
    for d in partners:
        pl.semaphore_signal(barrier, inc=1, device_id=d, device_id_type=MESH)

    def x_own(zp):
        cols = pl.ds(pl.multiple_of(((1 - yl) * 8 + zp) * 512 + yh * 256, 256), 256)
        return pltpu.make_async_copy(li.at[:, cols], xb.at[zp, pl.ds(0, 384)], xo_sem.at[zp])

    loads = [
        pltpu.make_async_copy(a, b, in_sem.at[i])
        for i, (a, b) in enumerate(((q_in, q), (k_in, k), (v_in, v), (do_in, do)))
    ]
    for load in loads:
        load.start()

    lens = [dl[0, i] for i in range(3)]
    ends = [lens[0], lens[0] + lens[1], lens[0] + lens[1] + lens[2]]

    def documents(shape, dim):
        pos = lax.broadcasted_iota(jnp.int32, shape, dim)
        return pos, sum((pos >= e).astype(jnp.int32) for e in ends)

    kpos, kdoc = documents((384, 1), 0)
    qpos, qdoc = documents((1, 384), 1)
    bias[...] = jnp.where((kdoc == qdoc) & (kpos <= qpos), 0.0, -1e30).astype(F32)
    scale = 1.0 / HD**0.5

    def value_pass(b):
        n = 128 * (b + 1)
        rows = pl.ds(128 * b, 128)
        total = None
        for h in range(HEADS):
            lanes = pl.ds(HD * h, HD)
            s = dot(k[:n], q[rows, lanes], ((1,), (1,))) + bias[:n, 128 * b:n]
            e = jnp.exp((s - jnp.max(s, axis=0, keepdims=True)) * scale)
            soft = e * (1.0 / jnp.sum(e, axis=0, keepdims=True))
            probs[h, :n, 128 * b:n] = soft
            term = dot(soft.astype(BF16), do[rows, lanes], ((1,), (0,)))
            total = term if total is None else total + term
        add_rows(vacc, n, total)

    def key_pass(b):
        n = 128 * (b + 1)
        rows = pl.ds(128 * b, 128)
        total = None
        for h in range(HEADS):
            lanes = pl.ds(HD * h, HD)
            soft = probs[h, :n, 128 * b:n]
            pg = dot(v[:n], do[rows, lanes], ((1,), (1,)))
            inner = jnp.sum(soft * pg, axis=0, keepdims=True)
            ds = (soft * (pg - inner) * scale).astype(BF16)
            qg[rows, lanes] = dot(ds, k[:n], ((0,), (0,))).astype(BF16)
            term = dot(ds, q[rows, lanes], ((1,), (0,)))
            total = term if total is None else total + term
        add_rows(kacc, n, total)

    def add_rows(acc, n, total):
        if n == 384:
            acc[...] = total
        else:
            acc[:n] += total

    for load in loads:
        load.wait()
    for b in (2, 1, 0):
        value_pass(b)

    pl.semaphore_wait(barrier, len(partners))

    rows_p = pl.ds(pl.multiple_of(p * 128, 128), 128)
    rows_o = pl.ds(pl.multiple_of((1 - p) * 128, 128), 128)

    def w0_rows(i):
        return w.at[pl.ds(pl.multiple_of(256 * i + p * 128, 128), 128)]

    def w0_remote(i):
        return remote(
            w0_rows(i), wz.at[z, yh], w0_s.at[i], w0_r.at[yh],
            device(x, 2 * yl + i, z, c),
        )

    def w0_local(i):
        return pltpu.make_async_copy(w0_rows(i), wz.at[z, yh], w0_r.at[yh])

    for i in range(2):
        @pl.when(2 * yl + i != y)
        def _():
            w0_remote(i).start()

        @pl.when(2 * yl + i == y)
        def _():
            w0_local(i).start()

    def x_send(side, zp):
        ydst = (y + 1) % 4 if side == 0 else (y + 3) % 4
        cols = pl.ds(pl.multiple_of((yl * 8 + zp) * 512 + (ydst // 2) * 256, 256), 256)
        return remote(
            li.at[pl.ds(192 * side, 192), cols],
            xb.at[zp, pl.ds(384 + 192 * side, 192)],
            xs_s.at[side, zp % 4], xs_r.at[side, zp % 4], device(x, ydst, z, c),
        )

    def x_relay(zp):
        ref = xb.at[zp, pl.ds(384, 384)]
        return remote(ref, ref, xsib_s.at[zp % 4], xsib_r.at[zp % 4], sibling)

    def block(dz):
        return (z + dz) % 8

    def x_start(*dzs):
        for dz in dzs:
            zp = block(dz)

            @pl.when(zp // 4 == c)
            def _():
                for side in range(2):
                    x_send(side, zp).start()

    for dz in BY_USE:
        x_own(block(dz)).start()

    def x_pass(dz):
        zp = block(dz)

        @pl.when(zp // 4 == c)
        def _():
            for side in range(2):
                x_send(side, zp).wait_recv()
            x_relay(zp).start()

    def x_ready(dz):
        zp = block(dz)
        x_own(zp).wait()

        @pl.when(zp // 4 != c)
        def _():
            x_relay(zp).wait_recv()

    def spread_x(zp, side):
        j, cz = zp % 4, zp // 4
        return remote(
            wz.at[zp, side], wfull.at[j, c, side, rows_p],
            wx_s.at[zp, side], wx_r.at[j, c, side],
            at(dx=1 if side == 0 else 3, core=cz),
        )

    def spread_sibling(zp):
        j = zp % 4
        return remote(
            wz.at[zp], wfull.at[j, c, :, rows_p], wsib_s.at[zp], wsib_r.at[j], sibling
        )

    def spread_local(zp):
        j = zp % 4
        return pltpu.make_async_copy(wz.at[zp], wfull.at[j, c, :, rows_p], wloc.at[j])

    def spread(zp):
        for side in range(2):
            spread_x(zp, side).start()

        @pl.when(zp // 4 == c)
        def _():
            spread_local(zp).start()

        @pl.when(zp // 4 != c)
        def _():
            spread_sibling(zp).start()

    def wz_copy(direction, s):
        zp = (z - s + 8) % 8 if direction == 0 else (z + s) % 8
        ref = wz.at[zp, direction] if s == 3 else wz.at[zp]
        return remote(
            ref, ref, wz_s.at[direction, s], wz_r.at[direction, s],
            at(dz=1 if direction == 0 else 7),
        )

    def wz_wait(direction, s):
        zp = (z - s + 7) % 8 if direction == 0 else (z + s + 1) % 8
        ref = wz.at[zp, direction] if s == 3 else wz.at[zp]
        remote(ref, ref, wz_s.at[direction, s], wz_r.at[direction, s], sibling).wait_recv()
        return zp

    def w_begin():
        for h in range(2):
            remote(w0_rows(0), wz.at[z, h], w0_s.at[h], w0_r.at[h], sibling).wait_recv()
        for direction in range(2):
            wz_copy(direction, 0).start()
        spread(z)

    def w_step(s):
        arrived = [wz_wait(direction, s) for direction in range(2)]
        if s < 3:
            for direction in range(2):
                wz_copy(direction, s + 1).start()
            for zp in arrived:
                spread(zp)
        else:
            spread(arrived[0])

    def part(i):
        return pl.ds(128 * (1 - i), 128)

    def kv1(i, side):
        return remote(
            kv_all.at[c, yh, :, part(i)], kv_oth.at[c, yh, :, part(i)],
            k1_s.at[i, side], k1_r.at[i, yh], at(dy=1 if side == 0 else 3),
        )

    def kv1_start(i, acc):
        kv_all[c, yh, :, part(i)] = acc[...].astype(BF16)
        for side in range(2):
            kv1(i, side).start()

    def kv2(i, side):
        hsrc = ((y + 3) % 4) // 2 if side == 0 else ((y + 1) % 4) // 2
        rows = pl.ds(192 * side, 192)
        return remote(
            kv_oth.at[c, hsrc, rows, part(i)], kv_all.at[c, hsrc, rows, part(i)],
            k2_s.at[i, side], k2_r.at[i, side], at(dy=1 if side == 0 else 3),
        )

    def transpose_kv(i, h):
        kvt[h, part(i), :384] = kv_all[c, h, :, part(i)].astype(F32).T.astype(BF16)
        kvt[h, part(i), 384:] = kv_oth[c, h, :, part(i)].astype(F32).T.astype(BF16)

    def kv1_ready(i):
        for h in range(2):
            remote(
                kv_oth.at[c, h, :, part(i)], kv_oth.at[c, h, :, part(i)],
                k1_s.at[i, h], k1_r.at[i, h], sibling,
            ).wait_recv()
        for side in range(2):
            kv2(i, side).start()
        transpose_kv(i, yh)

    def kv2_ready(i):
        for side in range(2):
            rows = pl.ds(192 * side, 192)
            ref = kv_all.at[c, 1 - yh, rows, part(i)]
            remote(ref, ref, k2_s.at[i, side], k2_r.at[i, side], sibling).wait_recv()
        transpose_kv(i, 1 - yh)

    def kv_sibling(i, core):
        ref = (kv_all.at[core, yh], kv_all.at[core, 1 - yh], kv_oth.at[core])[i]
        return remote(ref, ref, ks_s.at[i], ks_r.at[i], sibling)

    def bulk(f, *dzs):
        h = yh if f % 2 == 0 else 1 - yh
        first = 128 * (1 - f // 2)
        for dz in dzs:
            pt[f, dz] = dot(kvt[h, first:first + 128, :], xb[block(dz)], ((1,), (0,)))

    def rs_copy(f, direction, s):
        half = pl.ds(0, 64) if s == 0 else pl.ds(0, 128)
        return remote(
            sbuf.at[f, direction, s, half], rbuf.at[f, direction, s, half],
            rs_s.at[f, direction, s], rs_r.at[f, direction, s],
            at(dz=1 if direction == 0 else 7),
        )

    def rs_step(f, s):
        for direction in range(2):
            dz = 4 - s if direction == 0 else 4 + s
            if s == 0:
                mine = slice(64 * direction, 64 * direction + 64)
                sbuf[f, direction, 0, :64] = pt[f, 4, mine].astype(BF16)
            else:
                rs_copy(f, direction, s - 1).wait_recv()
                if s == 1:
                    mine = slice(64 * direction, 64 * direction + 64)
                    rest = slice(64 - 64 * direction, 128 - 64 * direction)
                    sbuf[f, direction, 1, rest] = pt[f, dz, rest].astype(BF16)
                    sbuf[f, direction, 1, mine] = (
                        pt[f, dz, mine] + rbuf[f, direction, 0, :64].astype(F32)
                    ).astype(BF16)
                else:
                    sbuf[f, direction, s] = (
                        pt[f, dz] + rbuf[f, direction, s - 1].astype(F32)
                    ).astype(BF16)
            rs_copy(f, direction, s).start()

    def rs_last(f):
        total = pt[f, 0]
        for direction in range(2):
            rs_copy(f, direction, 3).wait_recv()
            total = total + rbuf[f, direction, 3].astype(F32)
        facc[f // 2, f % 2] = total
        xs[f // 2, f % 2] = total.astype(BF16)

    def x_copy(i, n):
        quarter = pl.ds(pl.multiple_of(((x + n) % 4) * 32, 32), 32)
        return remote(
            xs.at[i, :, quarter], xr.at[i, n - 1], xr_s.at[i, n - 1], xr_r.at[i, n - 1],
            at(dx=n),
        )

    def x_first(i):
        for n in (2, 1, 3):
            x_copy(i, n).start()

    def fin_copy(i, slot, n):
        h = yh if slot == 0 else 1 - yh
        cols = pl.ds(pl.multiple_of(128 * (1 - i) + x * 32, 32), 32)
        return remote(
            fin.at[i, slot], wgt.at[yh, cols], fin_s.at[i, slot, n], fin_r.at[i, yh, x],
            device((x + n) % 4, 2 * h + 1 - yl, z, c),
        )

    def x_last(i):
        total = facc[i, :, pl.ds(pl.multiple_of(x * 32, 32), 32)]
        for n in range(1, 4):
            x_copy(i, n).wait_recv()
            total = total + xr[i, n - 1].astype(F32)
        fin[i] = total.astype(BF16)
        for n in (2, 1, 3, 0):
            for slot in range(2):
                fin_copy(i, slot, n).start()

    def w_ready(j):
        pltpu.make_async_copy(wz.at[0], wfull.at[j, c, :, rows_p], wloc.at[j]).wait()
        remote(
            wz.at[0], wfull.at[j, 1 - c, :, rows_p], wsib_s.at[0], wsib_r.at[j], sibling
        ).wait_recv()
        for cc in range(2):
            for side in range(2):
                remote(
                    wz.at[0, side], wfull.at[j, cc, side, rows_o],
                    wx_s.at[0, side], wx_r.at[j, cc, side], sibling,
                ).wait_recv()

    def ig_copy(j):
        return remote(
            igo.at[j], igi.at[j], ig_s.at[j], ig_r.at[j], device(x, 2 * yh + 1 - yl, z, c)
        )

    def rows_of(kv, j):
        total = None
        for cc in range(2):
            for h in range(2):
                term = dot(kv[cc, h], wfull[j, cc, h], ((1,), (1,)))
                total = term if total is None else total + term
        return total.astype(BF16)

    def ig_other(r):
        j = (z + r) % 4
        w_ready(j)
        igo[j] = rows_of(kv_oth, j)
        ig_copy(j).start()

    def ig_own(r):
        j = (z + r) % 4
        iga[j] = rows_of(kv_all, j)
        ig_store(j, 0).start()

    def ig_store(j, other):
        half = yl if other == 0 else 1 - yl
        cols = pl.ds(pl.multiple_of(512 * j + 256 * half, 256), 256)
        src = iga.at[j] if other == 0 else igi.at[j]
        return pltpu.make_async_copy(src, ig_out.at[:, cols], out_sem.at[2 * j + other])

    def ig_last(r):
        j = (z + r) % 4
        ig_copy(j).wait_recv()
        ig_store(j, 1).start()

    qg_store = pltpu.make_async_copy(qg, qg_out, out_sem.at[8])
    wg_store = pltpu.make_async_copy(wgt, wg_out, out_sem.at[9])

    kv1_start(0, vacc)
    x_start(4, 3, 5)
    key_pass(2)
    w_begin()
    key_pass(1)
    key_pass(0)
    kv1_start(1, kacc)
    qg_store.start()
    kv1_ready(0)
    x_start(2, 6, 1, 7, 0)
    kv_sibling(0, c).start()
    x_pass(4)
    x_pass(3)
    x_pass(5)
    w_step(0)
    x_ready(4)
    bulk(0, 4)
    rs_step(0, 0)
    kv2_ready(0)
    bulk(1, 4)
    rs_step(1, 0)
    x_ready(3)
    x_ready(5)
    bulk(0, 3, 5)
    rs_step(0, 1)
    bulk(1, 3, 5)
    kv1_ready(1)
    kv_sibling(2, c).start()
    w_step(1)
    bulk(2, 4, 3, 5)
    rs_step(2, 0)
    rs_step(1, 1)
    x_pass(2)
    x_pass(6)
    kv2_ready(1)
    kv_sibling(1, c).start()
    bulk(3, 4, 3, 5)
    rs_step(3, 0)
    x_pass(1)
    x_pass(7)
    x_pass(0)
    w_step(2)
    x_ready(2)
    x_ready(6)
    for f in range(4):
        bulk(f, 2, 6)
    rs_step(0, 2)
    rs_step(2, 1)
    kv_sibling(2, 1 - c).wait_recv()
    ig_other(1)
    rs_step(1, 2)
    ig_other(2)
    rs_step(3, 1)
    for dz in (1, 7, 0):
        x_ready(dz)
    for f in range(4):
        bulk(f, 1, 7, 0)
    rs_step(0, 3)
    ig_other(3)
    w_step(3)
    rs_step(2, 2)
    rs_step(1, 3)
    rs_last(0)
    rs_step(3, 2)
    ig_other(0)
    rs_step(2, 3)
    rs_last(1)
    x_first(0)
    rs_step(3, 3)
    for i in range(2):
        kv_sibling(i, 1 - c).wait_recv()
    ig_own(0)
    rs_last(2)
    ig_own(1)
    x_last(0)
    rs_last(3)
    x_first(1)
    ig_own(2)
    ig_own(3)
    for r in (1, 2, 3):
        ig_last(r)
    x_last(1)
    ig_last(0)

    for i in range(2):
        for hs in range(2):
            for xx in range(4):
                cols = pl.ds(128 * (1 - i) + 32 * xx, 32)
                remote(
                    fin.at[0, 0], wgt.at[hs, cols], fin_s.at[0, 0, 0], fin_r.at[i, hs, xx], sibling
                ).wait_recv()
    wg_store.start()

    for i in range(2):
        @pl.when(2 * yl + i != y)
        def _():
            w0_remote(i).wait_send()
    for side in range(2):
        for i in range(2):
            kv1(i, side).wait_send()
            kv2(i, side).wait_send()
        for s in range(4):
            wz_copy(side, s).wait_send()
            for f in range(4):
                rs_copy(f, side, s).wait_send()
    for i in range(3):
        kv_sibling(i, c).wait_send()
    for j in range(4):
        zp = 4 * c + j
        for side in range(2):
            x_send(side, zp).wait_send()
        x_relay(zp).wait_send()
        ig_copy(j).wait_send()
        for other in range(2):
            ig_store(j, other).wait()
    for zp in range(8):
        for side in range(2):
            spread_x(zp, side).wait_send()

        @pl.when(zp // 4 != c)
        def _():
            spread_sibling(zp).wait_send()
    for i in range(2):
        for n in range(1, 4):
            x_copy(i, n).wait_send()
        for slot in range(2):
            for n in range(4):
                fin_copy(i, slot, n).wait_send()
    qg_store.wait()
    wg_store.wait()


def finish(ig_in, qg_in, wgt_in, ig, qg, wg, igv, qgv, wgt, wgf, load, store):
    pieces = [
        (ig_in.at[pl.ds(96 * i, 96)], igv.at[pl.ds(96 * i, 96)], ig.at[pl.ds(96 * i, 96)])
        for i in range(4)
    ] + [
        (qg_in.at[pl.ds(192 * i, 192)], qgv.at[pl.ds(192 * i, 192)], qg.at[pl.ds(192 * i, 192)])
        for i in range(2)
    ]
    first = pltpu.make_async_copy(wgt_in, wgt, load.at[6])
    first.start()
    loads = [pltpu.make_async_copy(a, b, load.at[i]) for i, (a, b, _) in enumerate(pieces)]
    stores = [pltpu.make_async_copy(b, o, store.at[i]) for i, (_, b, o) in enumerate(pieces)]
    for copy in loads:
        copy.start()
    first.wait()
    for hs in range(2):
        wgf[256 * hs:256 * hs + 256, :] = wgt[hs].astype(F32).T
    last = pltpu.make_async_copy(wgf, wg, store.at[6])
    last.start()
    for a, b in zip(loads, stores):
        a.wait()
        b.start()
    for copy in stores:
        copy.wait()
    last.wait()


def shards(layer_input, queries, keys, values, kv_weight, out_grad, doc_lengths):
    hbm = pl.BlockSpec(memory_space=pl.ANY)
    smem = pl.BlockSpec(memory_space=pltpu.SMEM)
    dma = pltpu.SemaphoreType.DMA
    results = pl.pallas_call(
        kernel,
        out_shape=(
            jax.ShapeDtypeStruct((384, 2048), BF16),
            jax.ShapeDtypeStruct((384, 1024), BF16),
            jax.ShapeDtypeStruct((2, 256, 256), BF16),
        ),
        in_specs=[hbm, hbm, hbm, hbm, hbm, hbm, smem],
        out_specs=(hbm, hbm, hbm),
        scratch_shapes=[
            pltpu.VMEM((384, 1024), BF16),
            pltpu.VMEM((384, 128), BF16),
            pltpu.VMEM((384, 128), BF16),
            pltpu.VMEM((384, 1024), BF16),
            pltpu.VMEM((8, 384, 384), F32),
            pltpu.VMEM((384, 1024), BF16),
            pltpu.VMEM((8, 768, 256), BF16),
            pltpu.VMEM((8, 2, 128, 256), BF16),
            pltpu.VMEM((4, 2, 2, 256, 256), BF16),
            pltpu.VMEM((2, 2, 384, 256), BF16),
            pltpu.VMEM((2, 2, 384, 256), BF16),
            pltpu.VMEM((2, 256, 768), BF16),
            pltpu.VMEM((4, 2, 4, 128, 256), BF16),
            pltpu.VMEM((4, 2, 4, 128, 256), BF16),
            pltpu.VMEM((2, 2, 128, 256), F32),
            pltpu.VMEM((2, 2, 128, 256), BF16),
            pltpu.VMEM((2, 3, 2, 32, 256), BF16),
            pltpu.VMEM((2, 2, 32, 256), BF16),
            pltpu.VMEM((2, 256, 256), BF16),
            pltpu.VMEM((4, 384, 256), BF16),
            pltpu.VMEM((4, 384, 256), BF16),
            pltpu.VMEM((4, 384, 256), BF16),
            pltpu.VMEM((4, 8, 128, 256), F32),
            pltpu.VMEM((384, 384), F32),
            pltpu.VMEM((384, 128), F32),
            pltpu.VMEM((384, 128), F32),
            dma((4,)), dma((10,)), dma((8,)), dma((2, 4)), dma((2, 4)), dma((4,)), dma((4,)),
            dma((2,)), dma((2,)), dma((2, 4)), dma((2, 4)),
            dma((8, 2)), dma((4, 2, 2)), dma((8,)), dma((4,)), dma((4,)),
            dma((2, 2)), dma((2, 2)), dma((2, 2)), dma((2, 2)), dma((3,)), dma((3,)),
            dma((4, 2, 4)), dma((4, 2, 4)), dma((2, 3)), dma((2, 3)),
            dma((2, 2, 4)), dma((2, 2, 4)), dma((4,)), dma((4,)),
        ],
        compiler_params=pltpu.CompilerParams(
            collective_id=0, has_side_effects=True, vmem_limit_bytes=56 << 20
        ),
        cost_estimate=pl.CostEstimate(
            flops=5 * 10**9, bytes_accessed=2 * 10**7, transcendentals=10**6
        ),
        name="kv_back",
    )(layer_input, queries, keys, values, kv_weight, out_grad, doc_lengths)
    return pl.pallas_call(
        finish,
        out_shape=(
            jax.ShapeDtypeStruct((384, 2048), BF16),
            jax.ShapeDtypeStruct((384, 1024), BF16),
            jax.ShapeDtypeStruct((512, 256), F32),
        ),
        in_specs=[hbm, hbm, hbm],
        out_specs=(hbm, hbm, hbm),
        scratch_shapes=[
            pltpu.VMEM((384, 2048), BF16), pltpu.VMEM((384, 1024), BF16),
            pltpu.VMEM((2, 256, 256), BF16), pltpu.VMEM((512, 256), F32), dma((7,)), dma((7,)),
        ],
        compiler_params=pltpu.CompilerParams(vmem_limit_bytes=60 << 20),
        name="finish",
    )(*results)


def solution(mesh):
    placed = (
        P(("blk", "dp"), None),
        P(("blk", "dp"), "tp"),
        P(("blk", "dp"), "tp"),
        P(("blk", "dp"), "tp"),
        P("blk", "tp"),
        P(("blk", "dp"), "tp"),
        P(("blk", "dp"), None),
    )
    return jax.shard_map(
        shards,
        mesh=mesh,
        in_specs=placed,
        out_specs=(P(("blk", "dp"), "tp"), P(("blk", "dp"), "tp"), P("blk", "tp")),
        check_vma=False,
    )
```

```python
import functools

import jax
import jax.numpy as jnp
from jax import lax
from jax.experimental import pallas as pl
from jax.experimental.pallas import tpu as pltpu
from jax.sharding import PartitionSpec as P

HD = 128
HEADS = 8
BY_USE = (4, 3, 5, 2, 6, 1, 7, 0)
MESH = pl.DeviceIdType.MESH
F32 = jnp.float32
BF16 = jnp.bfloat16


def device(x, y, z, c):
    return {"blk": (y % 2) * 8 + z, "tp": (y // 2) * 2 + c, "dp": x}


def dot(a, b, dims):
    return lax.dot_general(a, b, (dims, ((), ())), preferred_element_type=F32)


def kernel(
    li, q_in, k_in, v_in, w, do_in, dl,
    ig_out, qg_out, wg_out,
    q, k, v, do, probs, qg, xb, wz, wfull, kv_all, kv_oth, kvt, sbuf, rbuf, facc, xs, xr, fin, wgt,
    iga, igo, igi, pt, bias, kacc, vacc,
    in_sem, out_sem, xo_sem, xs_s, xs_r, xsib_s, xsib_r,
    w0_s, w0_r, wz_s, wz_r, wx_s, wx_r, wsib_s, wsib_r, wloc,
    k1_s, k1_r, k2_s, k2_r, ks_s, ks_r,
    rs_s, rs_r, xr_s, xr_r, fin_s, fin_r, ig_s, ig_r,
):
    blk, tp, x = lax.axis_index("blk"), lax.axis_index("tp"), lax.axis_index("dp")
    yl, z, yh, c = blk // 8, blk % 8, tp // 2, tp % 2
    y = yh * 2 + yl
    p = x % 2

    def remote(src, dst, ssem, rsem, dev):
        return pltpu.make_async_remote_copy(
            src_ref=src, dst_ref=dst, send_sem=ssem, recv_sem=rsem,
            device_id=dev, device_id_type=MESH,
        )

    def at(dx=0, dy=0, dz=0, core=None):
        return device((x + dx) % 4, (y + dy) % 4, (z + dz) % 8, c if core is None else core)

    sibling = at(core=1 - c)

    partners = [at(dz=1), at(dz=7), sibling, at(dy=1), at(dy=2), at(dy=3), at(dx=2)]
    for dx in (1, 3):
        for core in (0, 1):
            partners.append(at(dx=dx, core=core))
    for dx in (1, 2, 3):
        for dy in (1, 3):
            partners.append(at(dx=dx, dy=dy))
    barrier = pltpu.get_barrier_semaphore()
    for d in partners:
        pl.semaphore_signal(barrier, inc=1, device_id=d, device_id_type=MESH)

    def x_own(zp):
        cols = pl.ds(pl.multiple_of(((1 - yl) * 8 + zp) * 512 + yh * 256, 256), 256)
        return pltpu.make_async_copy(li.at[:, cols], xb.at[zp, pl.ds(0, 384)], xo_sem.at[zp])

    loads = [
        pltpu.make_async_copy(a, b, in_sem.at[i])
        for i, (a, b) in enumerate(((q_in, q), (k_in, k), (v_in, v), (do_in, do)))
    ]
    for load in loads:
        load.start()

    lens = [dl[0, i] for i in range(3)]
    ends = [lens[0], lens[0] + lens[1], lens[0] + lens[1] + lens[2]]

    def documents(shape, dim):
        pos = lax.broadcasted_iota(jnp.int32, shape, dim)
        return pos, sum((pos >= e).astype(jnp.int32) for e in ends)

    kpos, kdoc = documents((384, 1), 0)
    qpos, qdoc = documents((1, 384), 1)
    bias[...] = jnp.where((kdoc == qdoc) & (kpos <= qpos), 0.0, -1e30).astype(F32)
    scale = 1.0 / HD**0.5

    def value_pass(b):
        n = 128 * (b + 1)
        rows = pl.ds(128 * b, 128)
        total = None
        for h in range(HEADS):
            lanes = pl.ds(HD * h, HD)
            s = dot(k[:n], q[rows, lanes], ((1,), (1,))) + bias[:n, 128 * b:n]
            e = jnp.exp((s - jnp.max(s, axis=0, keepdims=True)) * scale)
            soft = e * (1.0 / jnp.sum(e, axis=0, keepdims=True))
            probs[h, :n, 128 * b:n] = soft
            term = dot(soft.astype(BF16), do[rows, lanes], ((1,), (0,)))
            total = term if total is None else total + term
        add_rows(vacc, n, total)

    def key_pass(b):
        n = 128 * (b + 1)
        rows = pl.ds(128 * b, 128)
        total = None
        for h in range(HEADS):
            lanes = pl.ds(HD * h, HD)
            soft = probs[h, :n, 128 * b:n]
            pg = dot(v[:n], do[rows, lanes], ((1,), (1,)))
            inner = jnp.sum(soft * pg, axis=0, keepdims=True)
            ds = (soft * (pg - inner) * scale).astype(BF16)
            qg[rows, lanes] = dot(ds, k[:n], ((0,), (0,))).astype(BF16)
            term = dot(ds, q[rows, lanes], ((1,), (0,)))
            total = term if total is None else total + term
        add_rows(kacc, n, total)

    def add_rows(acc, n, total):
        if n == 384:
            acc[...] = total
        else:
            acc[:n] += total

    for load in loads:
        load.wait()
    for b in (2, 1, 0):
        value_pass(b)

    pl.semaphore_wait(barrier, len(partners))

    rows_p = pl.ds(pl.multiple_of(p * 128, 128), 128)
    rows_o = pl.ds(pl.multiple_of((1 - p) * 128, 128), 128)

    def w0_rows(i):
        return w.at[pl.ds(pl.multiple_of(256 * i + p * 128, 128), 128)]

    def w0_remote(i):
        return remote(
            w0_rows(i), wz.at[z, yh], w0_s.at[i], w0_r.at[yh],
            device(x, 2 * yl + i, z, c),
        )

    def w0_local(i):
        return pltpu.make_async_copy(w0_rows(i), wz.at[z, yh], w0_r.at[yh])

    for i in range(2):
        @pl.when(2 * yl + i != y)
        def _():
            w0_remote(i).start()

        @pl.when(2 * yl + i == y)
        def _():
            w0_local(i).start()

    def x_send(side, zp):
        ydst = (y + 1) % 4 if side == 0 else (y + 3) % 4
        cols = pl.ds(pl.multiple_of((yl * 8 + zp) * 512 + (ydst // 2) * 256, 256), 256)
        return remote(
            li.at[pl.ds(192 * side, 192), cols],
            xb.at[zp, pl.ds(384 + 192 * side, 192)],
            xs_s.at[side, zp % 4], xs_r.at[side, zp % 4], device(x, ydst, z, c),
        )

    def x_relay(zp):
        ref = xb.at[zp, pl.ds(384, 384)]
        return remote(ref, ref, xsib_s.at[zp % 4], xsib_r.at[zp % 4], sibling)

    def block(dz):
        return (z + dz) % 8

    def x_start(*dzs):
        for dz in dzs:
            zp = block(dz)

            @pl.when(zp // 4 == c)
            def _():
                for side in range(2):
                    x_send(side, zp).start()

    for dz in BY_USE:
        x_own(block(dz)).start()

    def x_pass(dz):
        zp = block(dz)

        @pl.when(zp // 4 == c)
        def _():
            for side in range(2):
                x_send(side, zp).wait_recv()
            x_relay(zp).start()

    def x_ready(dz):
        zp = block(dz)
        x_own(zp).wait()

        @pl.when(zp // 4 != c)
        def _():
            x_relay(zp).wait_recv()

    def spread_x(zp, side):
        j, cz = zp % 4, zp // 4
        return remote(
            wz.at[zp, side], wfull.at[j, c, side, rows_p],
            wx_s.at[zp, side], wx_r.at[j, c, side],
            at(dx=1 if side == 0 else 3, core=cz),
        )

    def spread_sibling(zp):
        j = zp % 4
        return remote(
            wz.at[zp], wfull.at[j, c, :, rows_p], wsib_s.at[zp], wsib_r.at[j], sibling
        )

    def spread_local(zp):
        j = zp % 4
        return pltpu.make_async_copy(wz.at[zp], wfull.at[j, c, :, rows_p], wloc.at[j])

    def spread(zp):
        for side in range(2):
            spread_x(zp, side).start()

        @pl.when(zp // 4 == c)
        def _():
            spread_local(zp).start()

        @pl.when(zp // 4 != c)
        def _():
            spread_sibling(zp).start()

    def wz_copy(direction, s):
        zp = (z - s + 8) % 8 if direction == 0 else (z + s) % 8
        ref = wz.at[zp, direction] if s == 3 else wz.at[zp]
        return remote(
            ref, ref, wz_s.at[direction, s], wz_r.at[direction, s],
            at(dz=1 if direction == 0 else 7),
        )

    def wz_wait(direction, s):
        zp = (z - s + 7) % 8 if direction == 0 else (z + s + 1) % 8
        ref = wz.at[zp, direction] if s == 3 else wz.at[zp]
        remote(ref, ref, wz_s.at[direction, s], wz_r.at[direction, s], sibling).wait_recv()
        return zp

    def w_begin():
        for h in range(2):
            remote(w0_rows(0), wz.at[z, h], w0_s.at[h], w0_r.at[h], sibling).wait_recv()
        for direction in range(2):
            wz_copy(direction, 0).start()
        spread(z)

    def w_step(s):
        arrived = [wz_wait(direction, s) for direction in range(2)]
        if s < 3:
            for direction in range(2):
                wz_copy(direction, s + 1).start()
            for zp in arrived:
                spread(zp)
        else:
            spread(arrived[0])

    def part(i):
        return pl.ds(128 * (1 - i), 128)

    def kv1(i, side):
        return remote(
            kv_all.at[c, yh, :, part(i)], kv_oth.at[c, yh, :, part(i)],
            k1_s.at[i, side], k1_r.at[i, yh], at(dy=1 if side == 0 else 3),
        )

    def kv1_start(i, acc):
        kv_all[c, yh, :, part(i)] = acc[...].astype(BF16)
        for side in range(2):
            kv1(i, side).start()

    def kv2(i, side):
        hsrc = ((y + 3) % 4) // 2 if side == 0 else ((y + 1) % 4) // 2
        rows = pl.ds(192 * side, 192)
        return remote(
            kv_oth.at[c, hsrc, rows, part(i)], kv_all.at[c, hsrc, rows, part(i)],
            k2_s.at[i, side], k2_r.at[i, side], at(dy=1 if side == 0 else 3),
        )

    def transpose_kv(i, h):
        kvt[h, part(i), :384] = kv_all[c, h, :, part(i)].astype(F32).T.astype(BF16)
        kvt[h, part(i), 384:] = kv_oth[c, h, :, part(i)].astype(F32).T.astype(BF16)

    def kv1_ready(i):
        for h in range(2):
            remote(
                kv_oth.at[c, h, :, part(i)], kv_oth.at[c, h, :, part(i)],
                k1_s.at[i, h], k1_r.at[i, h], sibling,
            ).wait_recv()
        for side in range(2):
            kv2(i, side).start()
        transpose_kv(i, yh)

    def kv2_ready(i):
        for side in range(2):
            rows = pl.ds(192 * side, 192)
            ref = kv_all.at[c, 1 - yh, rows, part(i)]
            remote(ref, ref, k2_s.at[i, side], k2_r.at[i, side], sibling).wait_recv()
        transpose_kv(i, 1 - yh)

    def kv_sibling(i, core):
        ref = (kv_all.at[core, yh], kv_all.at[core, 1 - yh], kv_oth.at[core])[i]
        return remote(ref, ref, ks_s.at[i], ks_r.at[i], sibling)

    def bulk(f, *dzs):
        h = yh if f % 2 == 0 else 1 - yh
        first = 128 * (1 - f // 2)
        for dz in dzs:
            pt[f, dz] = dot(kvt[h, first:first + 128, :], xb[block(dz)], ((1,), (0,)))

    def rs_copy(f, direction, s):
        half = pl.ds(0, 64) if s == 0 else pl.ds(0, 128)
        return remote(
            sbuf.at[f, direction, s, half], rbuf.at[f, direction, s, half],
            rs_s.at[f, direction, s], rs_r.at[f, direction, s],
            at(dz=1 if direction == 0 else 7),
        )

    def rs_step(f, s):
        for direction in range(2):
            dz = 4 - s if direction == 0 else 4 + s
            if s == 0:
                mine = slice(64 * direction, 64 * direction + 64)
                sbuf[f, direction, 0, :64] = pt[f, 4, mine].astype(BF16)
            else:
                rs_copy(f, direction, s - 1).wait_recv()
                if s == 1:
                    mine = slice(64 * direction, 64 * direction + 64)
                    rest = slice(64 - 64 * direction, 128 - 64 * direction)
                    sbuf[f, direction, 1, rest] = pt[f, dz, rest].astype(BF16)
                    sbuf[f, direction, 1, mine] = (
                        pt[f, dz, mine] + rbuf[f, direction, 0, :64].astype(F32)
                    ).astype(BF16)
                else:
                    sbuf[f, direction, s] = (
                        pt[f, dz] + rbuf[f, direction, s - 1].astype(F32)
                    ).astype(BF16)
            rs_copy(f, direction, s).start()

    def rs_last(f):
        total = pt[f, 0]
        for direction in range(2):
            rs_copy(f, direction, 3).wait_recv()
            total = total + rbuf[f, direction, 3].astype(F32)
        facc[f // 2, f % 2] = total
        xs[f // 2, f % 2] = total.astype(BF16)

    def x_copy(i, n):
        quarter = pl.ds(pl.multiple_of(((x + n) % 4) * 32, 32), 32)
        return remote(
            xs.at[i, :, quarter], xr.at[i, n - 1], xr_s.at[i, n - 1], xr_r.at[i, n - 1],
            at(dx=n),
        )

    def x_first(i):
        for n in (2, 1, 3):
            x_copy(i, n).start()

    def fin_copy(i, slot, n):
        h = yh if slot == 0 else 1 - yh
        cols = pl.ds(pl.multiple_of(128 * (1 - i) + x * 32, 32), 32)
        return remote(
            fin.at[i, slot], wgt.at[yh, cols], fin_s.at[i, slot, n], fin_r.at[i, yh, x],
            device((x + n) % 4, 2 * h + 1 - yl, z, c),
        )

    def x_last(i):
        total = facc[i, :, pl.ds(pl.multiple_of(x * 32, 32), 32)]
        for n in range(1, 4):
            x_copy(i, n).wait_recv()
            total = total + xr[i, n - 1].astype(F32)
        fin[i] = total.astype(BF16)
        for n in (2, 1, 3, 0):
            for slot in range(2):
                fin_copy(i, slot, n).start()

    def w_ready(j):
        pltpu.make_async_copy(wz.at[0], wfull.at[j, c, :, rows_p], wloc.at[j]).wait()
        remote(
            wz.at[0], wfull.at[j, 1 - c, :, rows_p], wsib_s.at[0], wsib_r.at[j], sibling
        ).wait_recv()
        for cc in range(2):
            for side in range(2):
                remote(
                    wz.at[0, side], wfull.at[j, cc, side, rows_o],
                    wx_s.at[0, side], wx_r.at[j, cc, side], sibling,
                ).wait_recv()

    def ig_copy(j):
        return remote(
            igo.at[j], igi.at[j], ig_s.at[j], ig_r.at[j], device(x, 2 * yh + 1 - yl, z, c)
        )

    def rows_of(kv, j):
        total = None
        for cc in range(2):
            for h in range(2):
                term = dot(kv[cc, h], wfull[j, cc, h], ((1,), (1,)))
                total = term if total is None else total + term
        return total.astype(BF16)

    def ig_other(r):
        j = (z + r) % 4
        w_ready(j)
        igo[j] = rows_of(kv_oth, j)
        ig_copy(j).start()

    def ig_own(r):
        j = (z + r) % 4
        iga[j] = rows_of(kv_all, j)
        ig_store(j, 0).start()

    def ig_store(j, other):
        half = yl if other == 0 else 1 - yl
        cols = pl.ds(pl.multiple_of(512 * j + 256 * half, 256), 256)
        src = iga.at[j] if other == 0 else igi.at[j]
        return pltpu.make_async_copy(src, ig_out.at[:, cols], out_sem.at[2 * j + other])

    def ig_last(r):
        j = (z + r) % 4
        ig_copy(j).wait_recv()
        ig_store(j, 1).start()

    qg_store = pltpu.make_async_copy(qg, qg_out, out_sem.at[8])
    wg_store = pltpu.make_async_copy(wgt, wg_out, out_sem.at[9])

    kv1_start(0, vacc)
    x_start(4, 3, 5)
    key_pass(2)
    w_begin()
    key_pass(1)
    key_pass(0)
    kv1_start(1, kacc)
    qg_store.start()
    kv1_ready(0)
    x_start(2, 6)
    kv_sibling(0, c).start()
    x_pass(4)
    x_pass(3)
    x_pass(5)
    w_step(0)
    x_ready(4)
    bulk(0, 4)
    rs_step(0, 0)
    kv2_ready(0)
    x_start(1, 7, 0)
    bulk(1, 4)
    rs_step(1, 0)
    x_ready(3)
    x_ready(5)
    bulk(0, 3, 5)
    rs_step(0, 1)
    bulk(1, 3, 5)
    kv1_ready(1)
    kv_sibling(2, c).start()
    w_step(1)
    bulk(2, 4, 3, 5)
    rs_step(2, 0)
    rs_step(1, 1)
    x_pass(2)
    x_pass(6)
    kv2_ready(1)
    kv_sibling(1, c).start()
    bulk(3, 4, 3, 5)
    rs_step(3, 0)
    x_pass(1)
    x_pass(7)
    x_pass(0)
    w_step(2)
    x_ready(2)
    x_ready(6)
    for f in range(4):
        bulk(f, 2, 6)
    rs_step(0, 2)
    rs_step(2, 1)
    rs_step(1, 2)
    kv_sibling(2, 1 - c).wait_recv()
    ig_other(2)
    rs_step(3, 1)
    ig_other(1)
    for dz in (1, 7, 0):
        x_ready(dz)
    for f in range(4):
        bulk(f, 1, 7, 0)
    rs_step(0, 3)
    ig_other(3)
    w_step(3)
    rs_step(2, 2)
    rs_step(1, 3)
    rs_last(0)
    rs_step(3, 2)
    ig_other(0)
    rs_step(2, 3)
    rs_last(1)
    x_first(0)
    rs_step(3, 3)
    for i in range(2):
        kv_sibling(i, 1 - c).wait_recv()
    ig_own(0)
    rs_last(2)
    ig_own(1)
    x_last(0)
    rs_last(3)
    x_first(1)
    ig_own(2)
    ig_own(3)
    for r in (2, 1, 3):
        ig_last(r)
    x_last(1)
    ig_last(0)

    for i in range(2):
        @pl.when(2 * yl + i != y)
        def _():
            w0_remote(i).wait_send()
    for side in range(2):
        for i in range(2):
            kv1(i, side).wait_send()
            kv2(i, side).wait_send()
        for s in range(4):
            wz_copy(side, s).wait_send()
            for f in range(4):
                rs_copy(f, side, s).wait_send()
    for i in range(3):
        kv_sibling(i, c).wait_send()
    for j in range(4):
        zp = 4 * c + j
        for side in range(2):
            x_send(side, zp).wait_send()
        x_relay(zp).wait_send()
        ig_copy(j).wait_send()
        for other in range(2):
            ig_store(j, other).wait()
    for zp in range(8):
        for side in range(2):
            spread_x(zp, side).wait_send()

        @pl.when(zp // 4 != c)
        def _():
            spread_sibling(zp).wait_send()
    for i in range(2):
        for n in range(1, 4):
            x_copy(i, n).wait_send()
    qg_store.wait()

    for i in range(2):
        for hs in range(2):
            for xx in range(4):
                cols = pl.ds(128 * (1 - i) + 32 * xx, 32)
                remote(
                    fin.at[0, 0], wgt.at[hs, cols], fin_s.at[0, 0, 0], fin_r.at[i, hs, xx], sibling
                ).wait_recv()
    wg_store.start()
    for i in range(2):
        for slot in range(2):
            for n in range(4):
                fin_copy(i, slot, n).wait_send()
    wg_store.wait()


def finish(ig_in, qg_in, wgt_in, ig, qg, wg, igv, qgv, wgt, wgf, load, store):
    pieces = [
        (ig_in.at[pl.ds(96 * i, 96)], igv.at[pl.ds(96 * i, 96)], ig.at[pl.ds(96 * i, 96)])
        for i in range(4)
    ] + [
        (qg_in.at[pl.ds(192 * i, 192)], qgv.at[pl.ds(192 * i, 192)], qg.at[pl.ds(192 * i, 192)])
        for i in range(2)
    ]
    first = pltpu.make_async_copy(wgt_in, wgt, load.at[6])
    first.start()
    loads = [pltpu.make_async_copy(a, b, load.at[i]) for i, (a, b, _) in enumerate(pieces)]
    stores = [pltpu.make_async_copy(b, o, store.at[i]) for i, (_, b, o) in enumerate(pieces)]
    for copy in loads:
        copy.start()
    first.wait()
    for hs in range(2):
        wgf[256 * hs:256 * hs + 256, :] = wgt[hs].astype(F32).T
    last = pltpu.make_async_copy(wgf, wg, store.at[6])
    last.start()
    for a, b in zip(loads, stores):
        a.wait()
        b.start()
    for copy in stores:
        copy.wait()
    last.wait()


def shards(layer_input, queries, keys, values, kv_weight, out_grad, doc_lengths):
    hbm = pl.BlockSpec(memory_space=pl.ANY)
    smem = pl.BlockSpec(memory_space=pltpu.SMEM)
    dma = pltpu.SemaphoreType.DMA
    results = pl.pallas_call(
        kernel,
        out_shape=(
            jax.ShapeDtypeStruct((384, 2048), BF16),
            jax.ShapeDtypeStruct((384, 1024), BF16),
            jax.ShapeDtypeStruct((2, 256, 256), BF16),
        ),
        in_specs=[hbm, hbm, hbm, hbm, hbm, hbm, smem],
        out_specs=(hbm, hbm, hbm),
        scratch_shapes=[
            pltpu.VMEM((384, 1024), BF16),
            pltpu.VMEM((384, 128), BF16),
            pltpu.VMEM((384, 128), BF16),
            pltpu.VMEM((384, 1024), BF16),
            pltpu.VMEM((8, 384, 384), F32),
            pltpu.VMEM((384, 1024), BF16),
            pltpu.VMEM((8, 768, 256), BF16),
            pltpu.VMEM((8, 2, 128, 256), BF16),
            pltpu.VMEM((4, 2, 2, 256, 256), BF16),
            pltpu.VMEM((2, 2, 384, 256), BF16),
            pltpu.VMEM((2, 2, 384, 256), BF16),
            pltpu.VMEM((2, 256, 768), BF16),
            pltpu.VMEM((4, 2, 4, 128, 256), BF16),
            pltpu.VMEM((4, 2, 4, 128, 256), BF16),
            pltpu.VMEM((2, 2, 128, 256), F32),
            pltpu.VMEM((2, 2, 128, 256), BF16),
            pltpu.VMEM((2, 3, 2, 32, 256), BF16),
            pltpu.VMEM((2, 2, 32, 256), BF16),
            pltpu.VMEM((2, 256, 256), BF16),
            pltpu.VMEM((4, 384, 256), BF16),
            pltpu.VMEM((4, 384, 256), BF16),
            pltpu.VMEM((4, 384, 256), BF16),
            pltpu.VMEM((4, 8, 128, 256), F32),
            pltpu.VMEM((384, 384), F32),
            pltpu.VMEM((384, 128), F32),
            pltpu.VMEM((384, 128), F32),
            dma((4,)), dma((10,)), dma((8,)), dma((2, 4)), dma((2, 4)), dma((4,)), dma((4,)),
            dma((2,)), dma((2,)), dma((2, 4)), dma((2, 4)),
            dma((8, 2)), dma((4, 2, 2)), dma((8,)), dma((4,)), dma((4,)),
            dma((2, 2)), dma((2, 2)), dma((2, 2)), dma((2, 2)), dma((3,)), dma((3,)),
            dma((4, 2, 4)), dma((4, 2, 4)), dma((2, 3)), dma((2, 3)),
            dma((2, 2, 4)), dma((2, 2, 4)), dma((4,)), dma((4,)),
        ],
        compiler_params=pltpu.CompilerParams(
            collective_id=0, has_side_effects=True, vmem_limit_bytes=56 << 20
        ),
        cost_estimate=pl.CostEstimate(
            flops=5 * 10**9, bytes_accessed=2 * 10**7, transcendentals=10**6
        ),
        name="kv_back",
    )(layer_input, queries, keys, values, kv_weight, out_grad, doc_lengths)
    return pl.pallas_call(
        finish,
        out_shape=(
            jax.ShapeDtypeStruct((384, 2048), BF16),
            jax.ShapeDtypeStruct((384, 1024), BF16),
            jax.ShapeDtypeStruct((512, 256), F32),
        ),
        in_specs=[hbm, hbm, hbm],
        out_specs=(hbm, hbm, hbm),
        scratch_shapes=[
            pltpu.VMEM((384, 2048), BF16), pltpu.VMEM((384, 1024), BF16),
            pltpu.VMEM((2, 256, 256), BF16), pltpu.VMEM((512, 256), F32), dma((7,)), dma((7,)),
        ],
        compiler_params=pltpu.CompilerParams(vmem_limit_bytes=60 << 20),
        name="finish",
    )(*results)


def solution(mesh):
    placed = (
        P(("blk", "dp"), None),
        P(("blk", "dp"), "tp"),
        P(("blk", "dp"), "tp"),
        P(("blk", "dp"), "tp"),
        P("blk", "tp"),
        P(("blk", "dp"), "tp"),
        P(("blk", "dp"), None),
    )
    return jax.shard_map(
        shards,
        mesh=mesh,
        in_specs=placed,
        out_specs=(P(("blk", "dp"), "tp"), P(("blk", "dp"), "tp"), P("blk", "tp")),
        check_vma=False,
    )
```
